128 devices in a mesh: dp: 32 (over y, z_lo, x), rep: 4 (over z_hi, core).
Axes of the slice: x: 4, y: 4, z: 4 (z_hi: 2, z_lo: 2; z = z_hi * 2 + z_lo), core: 2. Of those that a mesh axis runs over, the one named last changes fastest.
Arguments:
- hidden_in: bfloat16 [98304, 4096], P(('dp', 'rep'))
- value_grad: bfloat16 [98304, 512], P(('dp', 'rep')), may hold values from -0.375 to 0.375
- value_weight: bfloat16 [4096, 512], replicated, may hold values from -0.09375 to 0.09375
- norm_gain: bfloat16 [4096], replicated, may hold values from 0.5 to 1.5
- owner_map: int32 [2], replicated, may hold values from 0 to 31, as said below
- mat_first: float32 [32, 4096, 512], P('dp', 'rep'), may hold values from -4 to 4
- mat_second: float32 [32, 4096, 512], P('dp', 'rep'), may hold values from 0.05 to 2
- vec_first: float32 [32, 4096], P('dp', 'rep'), may hold values from -4 to 4
- vec_second: float32 [32, 4096], P('dp', 'rep'), may hold values from 0.05 to 2
- next_hidden: bfloat16 [98304, 4096], P(('dp', 'rep'))
Outputs:
- new_weight: bfloat16 [4096, 512], replicated
- new_gain: bfloat16 [4096], replicated
- new_mat_first: float32 [32, 4096, 512], P('dp', 'rep')
- new_mat_second: float32 [32, 4096, 512], P('dp', 'rep')
- new_vec_first: float32 [32, 4096], P('dp', 'rep')
- new_vec_second: float32 [32, 4096], P('dp', 'rep')
- next_values: bfloat16 [98304, 512], P(('dp', 'rep'))
The draws below stay inside these ranges and needn't reach their ends.
Inputs may be any that keep to these rules, and one draw needn't show every extreme that they name: `owner_map`: entry 0 names the owner of the value projection, entry 1 the owner of the norm gain; the two differ, and one of them is 31.
All inputs are finite; a program needn't handle non-finite values.
Results may differ from the reference program's by a relative error of at most 0.0013.
The reference program's roundings to bfloat16 on the way count: a program that leaves them out, or rounds other values in their place, can miss the bound.
Values may be sent and summed in bfloat16 or wider, within the bound.
No kernel may reach another device: no remote copies, remote signals or barrier semaphores. Data moves between devices by JAX's collectives and lax.ppermute only.
A program may use at most 128 MiB of HBM per device.

```python
import math
import jax
import jax.numpy as jnp
from jax import lax

D = 4096
KV = 512
TOK_DEV = 768
TOKENS = 98304
N_DP = 32


def shaped_rows(key, values, upper_scale):
    key_row, key_col = jax.random.split(key, 2)
    row_scale = jnp.exp(jax.random.uniform(key_row, (TOKENS, 1), jnp.float32, 0.0, math.log(upper_scale)))
    col_scale = jnp.exp(jax.random.uniform(key_col, (1, D), jnp.float32, 0.0, math.log(upper_scale)))
    return values * row_scale * col_scale


def draw_hidden_in(key, part):
    key = jax.random.fold_in(key, 11)
    key_val, key_rest = jax.random.split(key, 2)
    values = jnp.clip(jax.random.normal(key_val, (TOKENS, D), jnp.float32), -6.0, 6.0)
    return shaped_rows(key_rest, values, 10.0).astype(jnp.bfloat16)


def draw_next_hidden(key, part):
    key = jax.random.fold_in(key, 23)
    key_val, key_rest = jax.random.split(key, 2)
    values = jnp.clip(jax.random.normal(key_val, (TOKENS, D), jnp.float32), -6.0, 6.0)
    return shaped_rows(key_rest, values, 10.0).astype(jnp.bfloat16)


def draw_owner_map(key, part):
    key = jax.random.fold_in(key, 5)
    key_other, key_flip = jax.random.split(key, 2)
    last_owner = jnp.int32(N_DP - 1)
    other_owner = jax.random.randint(key_other, (), 0, N_DP - 1).astype(jnp.int32)
    flip = jax.random.randint(key_flip, (), 0, 2).astype(jnp.int32)
    first_entry = jnp.where(flip == 1, last_owner, other_owner)
    second_entry = jnp.where(flip == 1, other_owner, last_owner)
    return jnp.stack([first_entry, second_entry]).astype(jnp.int32)


def block_levels(rng, shape, shards, smallest, largest):
    factor_of, own = 1.0, jax.random.fold_in(rng, 6)
    for axis_at, parts in shards:
        draws = jnp.exp(jax.random.uniform(jax.random.fold_in(own, axis_at), (parts,), jnp.float32, smallest / len(shards), largest / len(shards)))
        factor_of = factor_of * jnp.repeat(draws, shape[axis_at] // parts).reshape([-1 if axis == axis_at else 1 for axis in range(len(shape))])
    return factor_of


def noise(own_key, extent, deviation, reach, cuts=(), dtype=jnp.bfloat16):
    values = deviation * jax.random.normal(own_key, extent, jnp.float32)
    if cuts:
        values = values * block_levels(own_key, extent, cuts, -0.22, 0.18)
    return jnp.clip(values, -reach, reach).astype(dtype)


def setup_inputs(seed: int = 0) -> dict:
    arg_keys = jax.random.split(jax.random.key(seed), 11)
    return {
        "hidden_in": draw_hidden_in(jax.random.fold_in(arg_keys[10], 71), 0),
        "value_grad": noise(arg_keys[1], (TOKENS, KV), (8.0 * TOKENS ** -0.5), 0.375, ((0, 128),)),
        "value_weight": noise(arg_keys[2], (D, KV), D ** -0.5, 0.09375),
        "norm_gain": jnp.clip(1.0 + 0.1 * jax.random.normal(arg_keys[3], (D,), jnp.float32), 0.5, 1.5).astype(jnp.bfloat16),
        "owner_map": draw_owner_map(jax.random.fold_in(arg_keys[10], 71), 0),
        "mat_first": noise(arg_keys[5], (N_DP, D, KV), 0.3, 4.0, ((0, 32), (1, 4)), jnp.float32),
        "mat_second": jnp.clip(jnp.exp(math.log(2.0) - 3.6888794 * jax.random.uniform(arg_keys[6], (N_DP, D, KV), jnp.float32) ** block_levels(arg_keys[6], (N_DP, D, KV), ((0, 32), (1, 4)), -0.2, 0.2)), 0.05, 2.0),
        "vec_first": noise(arg_keys[7], (N_DP, D), 0.3, 4.0, ((0, 32), (1, 4)), jnp.float32),
        "vec_second": jnp.clip(jnp.exp(math.log(2.0) - 3.6888794 * jax.random.uniform(arg_keys[8], (N_DP, D), jnp.float32) ** block_levels(arg_keys[8], (N_DP, D), ((0, 32), (1, 4)), -0.2, 0.2)), 0.05, 2.0),
        "next_hidden": draw_next_hidden(jax.random.fold_in(arg_keys[10], 71), 0),
    }


norm_eps = 1e-05
adam_eps = 1e-08
beta_first = 0.9
beta_second = 0.95
learn_rate = 0.001
gain_rate = 0.02
fix_first = 1.0 - 0.9 ** 10
fix_second = 1.0 - 0.95 ** 10

def normalize(token_rows, gain_vec):
    widened = token_rows.astype(jnp.float32)
    inv_rms = lax.rsqrt(lax.optimization_barrier(jnp.mean(widened * widened, axis=-1, keepdims=True)) + norm_eps)
    unit_rows = widened * inv_rms
    return (unit_rows, (unit_rows * gain_vec.astype(jnp.float32)).astype(jnp.bfloat16))

def adam_step(parameter, gradient, first_moment, second_moment, step_rate):
    first_moment = beta_first * first_moment + (1.0 - beta_first) * gradient
    second_moment = beta_second * second_moment + (1.0 - beta_second) * gradient * gradient
    update = first_moment / fix_first / (jnp.sqrt(second_moment / fix_second) + adam_eps)
    return ((parameter.astype(jnp.float32) - step_rate * update).astype(jnp.bfloat16), first_moment, second_moment)

def reference(hidden_in, value_grad, value_weight, norm_gain, owner_map, mat_first, mat_second, vec_first, vec_second, next_hidden):
    block_count = TOKENS // TOK_DEV
    blocks_in = hidden_in.reshape(block_count, TOK_DEV, D)
    blocks_grad = value_grad.reshape(block_count, TOK_DEV, KV)

    def accumulate(running, block_pair):
        token_rows, upstream = block_pair
        unit_rows, normed = normalize(token_rows, norm_gain)
        weight_part = jnp.dot(normed.T, upstream, preferred_element_type=jnp.float32)
        input_grad = jnp.dot(upstream, value_weight.T, preferred_element_type=jnp.float32)
        return ((running[0] + weight_part, running[1] + lax.optimization_barrier(jnp.sum(input_grad * unit_rows, axis=0))), None)
    zero_sums = (jnp.zeros((D, KV), jnp.float32), jnp.zeros((D,), jnp.float32))
    sums, unused = lax.scan(accumulate, zero_sums, (blocks_in, blocks_grad))
    grad_weight, grad_gain = sums
    owner_weight = owner_map[0]
    owner_gain = owner_map[1]
    new_weight, first_weight, second_weight = adam_step(value_weight, grad_weight, mat_first[owner_weight], mat_second[owner_weight], learn_rate)
    new_gain, first_gain, second_gain = adam_step(norm_gain, grad_gain, vec_first[owner_gain], vec_second[owner_gain], gain_rate)
    new_mat_first = mat_first.at[owner_weight].set(first_weight)
    new_mat_second = mat_second.at[owner_weight].set(second_weight)
    new_vec_first = vec_first.at[owner_gain].set(first_gain)
    new_vec_second = vec_second.at[owner_gain].set(second_gain)

    def project(token_rows):
        unit_rows, normed = normalize(token_rows, new_gain)
        return jnp.dot(normed, new_weight, preferred_element_type=jnp.float32).astype(jnp.bfloat16)
    next_values = lax.map(project, next_hidden.reshape(block_count, TOK_DEV, D)).reshape(TOKENS, KV)
    return (new_weight, new_gain, new_mat_first, new_mat_second, new_vec_first, new_vec_second, next_values)
```

```python
import jax
import jax.numpy as jnp
from jax import lax
from jax.experimental import pallas as pl
from jax.experimental.pallas import tpu as pltpu
from jax.sharding import Mesh, PartitionSpec as P

norm_eps = 1e-05
adam_eps = 1e-08
beta_first = 0.9
beta_second = 0.95
learn_rate = 0.001
gain_rate = 0.02
fix_first = 1.0 - 0.9**10
fix_second = 1.0 - 0.95**10

D, KV, TOK = 4096, 512, 768
BLK = 512
AXES = ("y", "zl", "x", "zh", "c")
CHIPS = ("zh", "y", "zl", "x")
PARAMS = pltpu.CompilerParams(vmem_limit_bytes=50 * 1024 * 1024)
LINKS = (1, 8, 4, 3, 24, 36)
DP_LINKS = (1, 8, 4, 3, 24)


def pairs(mask, core=0):
    out = []
    for dev in range(128):
        chip = ((dev >> 1) & 1) * 32 + (dev >> 2)
        to = chip ^ mask
        out.append((dev, ((to & 31) << 2) + ((to >> 5) << 1) + ((dev & 1) ^ core)))
    return out


def swap(block, mask, core=0):
    return lax.ppermute(block, AXES, pairs(mask, core))


def adam_step(parameter, gradient, first_moment, second_moment, step_rate):
    first_moment = beta_first * first_moment + (1.0 - beta_first) * gradient
    second_moment = beta_second * second_moment + (1.0 - beta_second) * gradient * gradient
    update = first_moment / fix_first / (jnp.sqrt(second_moment / fix_second) + adam_eps)
    return (
        (parameter.astype(jnp.float32) - step_rate * update).astype(jnp.bfloat16),
        first_moment,
        second_moment,
    )


def fold(values):
    total = values[:, :128]
    for at in range(128, values.shape[1], 128):
        total = total + values[:, at : at + 128]
    return total


def grad_half(core, hid, gain, grad, inv, out):
    for at in range(4):
        start = ((at // 2) * 2 + core) * 1024 + (at % 2) * BLK
        cols = pl.ds(pl.multiple_of(start, BLK), BLK)
        unit = hid[:, cols].astype(jnp.float32) * inv
        normed = (unit * gain[:, cols].astype(jnp.float32)).astype(jnp.bfloat16)
        out[at // 2, pl.ds((at % 2) * BLK, BLK), :] = lax.dot_general(
            normed, grad, (((0,), (0,)), ((), ())), preferred_element_type=jnp.float32
        )


def send_kernel(core_ref, hid, gain, grad, out, inv_out):
    squares = jnp.zeros((TOK, 128), jnp.float32)
    for at in range(0, D, BLK):
        wide = hid[:, at : at + BLK].astype(jnp.float32)
        squares = squares + fold(wide * wide)
    mean = jnp.sum(squares, axis=1, keepdims=True) * (1.0 / D)
    inv = lax.rsqrt(mean + norm_eps)
    inv_out[...] = jnp.broadcast_to(inv, (TOK, 128))
    grad_half(1 - core_ref[0], hid, gain, grad[...], inv, out)


def keep_kernel(core_ref, hid, gain, grad, inv_ref, out):
    grad_half(core_ref[0], hid, gain, grad[...], inv_ref[:, :1], out)


def gain_kernel(hid, grad, weight, inv_ref, out):
    inv = inv_ref[:, :1]
    for at in range(0, D, BLK):
        back = lax.dot_general(
            grad[...],
            weight[at : at + BLK, :],
            (((1,), (1,)), ((), ())),
            preferred_element_type=jnp.float32,
        )
        unit = hid[:, at : at + BLK].astype(jnp.float32) * inv
        out[:, at : at + BLK] = jnp.sum(back * unit, axis=0, keepdims=True)


def norm_kernel(hid, gain, out):
    rows = hid.shape[0]
    squares = jnp.zeros((rows, 128), jnp.float32)
    for at in range(0, D, BLK):
        wide = hid[:, at : at + BLK].astype(jnp.float32)
        squares = squares + fold(wide * wide)
    inv = lax.rsqrt(jnp.sum(squares, axis=1, keepdims=True) * (1.0 / D) + norm_eps)
    for at in range(0, D, BLK):
        unit = hid[:, at : at + BLK].astype(jnp.float32) * inv
        scale = gain[:, at : at + BLK].astype(jnp.float32)
        out[:, at : at + BLK] = (unit * scale).astype(jnp.bfloat16)


def masks_of(order):
    masks = [0]
    for link in order:
        masks = masks + [m ^ link for m in masks]
    return masks


def turned(links, start):
    return links[start:] + links[:start]


PART_ORDER = tuple(turned(LINKS, p) for p in range(4))
SUM_ORDER = tuple(turned(DP_LINKS, 2 * p) for p in range(2))


def value_kernel(where_ref, *refs):
    own, other = refs[:4], refs[4:8]
    normed, weight, values = refs[8:]
    chip, core = where_ref[0], where_ref[1]
    for parts, side in ((own, core), (other, 1 - core)):
        for p in range(4):
            for j, mask in enumerate(masks_of(PART_ORDER[p])):
                to = lax.bitwise_xor(chip, mask)
                row = ((to >> 5) * 2 + side) * 1024 + lax.bitwise_and(to, 31) * 32
                weight[pl.ds(pl.multiple_of(row, 32), 32), p * 128 : p * 128 + 128] = parts[p][
                    j * 32 : j * 32 + 32, :
                ]
    values[...] = jnp.dot(
        normed[...], weight[...], preferred_element_type=jnp.float32
    ).astype(jnp.bfloat16)


def moment_kernel(where_ref, left, right, first, second, new_first, new_second):
    chip = where_ref[0]
    holds = where_ref[2] == 1
    new_first[...] = first[...]
    new_second[...] = second[...]

    @pl.when(holds)
    def _():
        for p, part in enumerate((left, right)):
            for j, mask in enumerate(masks_of(SUM_ORDER[p])):
                row = lax.bitwise_and(lax.bitwise_xor(chip, mask), 31) * 32
                at = (pl.ds(pl.multiple_of(row, 32), 32), slice(p * 256, p * 256 + 256))
                grad = part[j * 32 : j * 32 + 32, :]
                new_first[at] = beta_first * first[at] + (1.0 - beta_first) * grad
                new_second[at] = beta_second * second[at] + (1.0 - beta_second) * grad * grad


def vmem(n):
    return [pl.BlockSpec(memory_space=pltpu.VMEM)] * n


def smem():
    return [pl.BlockSpec(memory_space=pltpu.SMEM)]


def shape(dims, dtype):
    return jax.ShapeDtypeStruct(dims, dtype)


def body(
    hidden_in,
    value_grad,
    value_weight,
    norm_gain,
    owner_map,
    mat_first,
    mat_second,
    vec_first,
    vec_second,
    next_hidden,
):
    f32, bf16 = jnp.float32, jnp.bfloat16
    y, zl, x = lax.axis_index("y"), lax.axis_index("zl"), lax.axis_index("x")
    zh, core = lax.axis_index("zh"), lax.axis_index("c")
    place = y * 8 + zl * 4 + x
    rep = zh * 2 + core
    owner_weight, owner_gain = owner_map[0], owner_map[1]
    holds_weight = place == owner_weight
    holds_gain = place == owner_gain
    where = jnp.stack([zh * 32 + place, core, holds_weight.astype(jnp.int32)])
    core_at = core.reshape(1)
    gain_row = norm_gain.reshape(1, D)

    moments = jnp.stack([mat_first[0], mat_second[0]]).astype(jnp.float16)
    moments = moments.reshape(2, 4, 2, 4, 32, KV)

    def share(block, axis, at, source, unit):
        def pick(k):
            return lax.dynamic_index_in_dim(block, at ^ k, axis, keepdims=False)

        kept = pick(0)
        for k in range(1, block.shape[axis]):
            got = swap(pick(k), k * unit)
            kept = jnp.where((at ^ k) == source, got, kept)
        return kept

    moments = share(moments, 1, y, owner_weight >> 3, 8)
    moments = share(moments, 2, x, owner_weight & 3, 1)
    moments = share(moments, 1, zl, (owner_weight >> 2) & 1, 4)
    moments = moments.astype(f32)

    send, inv = pl.pallas_call(
        send_kernel,
        out_shape=(shape((2, 1024, KV), f32), shape((TOK, 128), f32)),
        in_specs=smem() + vmem(3),
        out_specs=tuple(vmem(2)),
        compiler_params=PARAMS,
    )(core_at, hidden_in, gain_row, value_grad)
    got = swap(send, 0, 1)
    keep = pl.pallas_call(
        keep_kernel,
        out_shape=shape((2, 1024, KV), f32),
        in_specs=smem() + vmem(4),
        out_specs=vmem(1)[0],
        compiler_params=PARAMS,
    )(core_at, hidden_in, gain_row, value_grad, inv)
    gain_part = pl.pallas_call(
        gain_kernel,
        out_shape=shape((1, D), f32),
        in_specs=vmem(4),
        out_specs=vmem(1)[0],
        compiler_params=PARAMS,
    )(hidden_in, value_grad, value_weight, inv)

    rows = jnp.arange(4)[:, None] == rep
    spread = [
        jnp.where(holds_gain & rows, vec[0][None, :], 0.0).reshape(32, 128)
        for vec in (vec_first, vec_second)
    ]
    sums = jnp.concatenate([gain_part.reshape(32, 128)] + spread)
    for mask in LINKS:
        sums = sums + swap(sums, mask)
    sums = sums + swap(sums, 0, 1)
    grad_gain, old_first, old_second = sums.reshape(3, D)
    new_gain, first_gain, second_gain = adam_step(
        norm_gain, grad_gain, old_first, old_second, gain_rate
    )
    first_rows = lax.dynamic_slice_in_dim(first_gain, rep * 1024, 1024)
    second_rows = lax.dynamic_slice_in_dim(second_gain, rep * 1024, 1024)
    new_vec_first = jnp.where(holds_gain, first_rows, vec_first[0])[None]
    new_vec_second = jnp.where(holds_gain, second_rows, vec_second[0])[None]

    chip_sum = (keep + got).reshape(64 * 32, KV)
    parts = lax.all_to_all(chip_sum, CHIPS, 0, 0, tiled=True)
    grad_rows = jnp.sum(parts.reshape(64, 32, KV), axis=0)

    own_rows = lax.dynamic_slice_in_dim(value_weight, rep * 1024 + place * 32, 32)
    weight_rows = adam_step(own_rows, grad_rows, moments[0], moments[1], learn_rate)[0]

    blocks = [weight_rows[:, p * 128 : p * 128 + 128] for p in range(4)]
    for step in range(6):
        blocks = [
            jnp.concatenate([block, swap(block, PART_ORDER[p][step])])
            for p, block in enumerate(blocks)
        ]
    others = [swap(block, 0, 1) for block in blocks]

    grads = [grad_rows[:, p * 256 : p * 256 + 256] for p in range(2)]
    for step in range(5):
        grads = [
            jnp.concatenate([block, swap(block, SUM_ORDER[p][step])])
            for p, block in enumerate(grads)
        ]

    next_normed = pl.pallas_call(
        norm_kernel,
        grid=(6,),
        out_shape=shape((TOK, D), bf16),
        in_specs=[
            pl.BlockSpec((128, D), lambda i: (i, 0)),
            pl.BlockSpec((1, D), lambda i: (0, 0)),
        ],
        out_specs=pl.BlockSpec((128, D), lambda i: (i, 0)),
        compiler_params=PARAMS,
    )(next_hidden, new_gain.reshape(1, D))

    new_weight, next_values = pl.pallas_call(
        value_kernel,
        out_shape=(shape((D, KV), bf16), shape((TOK, KV), bf16)),
        in_specs=smem() + vmem(9),
        out_specs=tuple(vmem(2)),
        compiler_params=PARAMS,
    )(where, *blocks, *others, next_normed)

    new_mat_first, new_mat_second = pl.pallas_call(
        moment_kernel,
        out_shape=(shape((1024, KV), f32), shape((1024, KV), f32)),
        in_specs=smem() + vmem(4),
        out_specs=tuple(vmem(2)),
        compiler_params=PARAMS,
    )(where, *grads, mat_first[0], mat_second[0])
    return (
        new_weight,
        new_gain,
        new_mat_first[None],
        new_mat_second[None],
        new_vec_first,
        new_vec_second,
        next_values,
    )


def solution(mesh):
    fine = Mesh(mesh.devices.reshape(4, 2, 4, 2, 2), AXES)
    dp, rep = ("y", "zl", "x"), ("zh", "c")
    tokens = P(AXES, None)
    return jax.shard_map(
        body,
        mesh=fine,
        in_specs=(
            tokens,
            tokens,
            P(),
            P(),
            P(),
            P(dp, rep, None),
            P(dp, rep, None),
            P(dp, rep),
            P(dp, rep),
            tokens,
        ),
        out_specs=(
            P(),
            P(),
            P(dp, rep, None),
            P(dp, rep, None),
            P(dp, rep),
            P(dp, rep),
            tokens,
        ),
        check_vma=False,
    )
```

```python
import jax
import jax.numpy as jnp
from jax import lax
from jax.experimental import pallas as pl
from jax.experimental.pallas import tpu as pltpu
from jax.sharding import Mesh, PartitionSpec as P

norm_eps = 1e-05
adam_eps = 1e-08
beta_first = 0.9
beta_second = 0.95
learn_rate = 0.001
gain_rate = 0.02
fix_first = 1.0 - 0.9**10
fix_second = 1.0 - 0.95**10

D, KV, TOK = 4096, 512, 768
BLK = 512
HALF = D // 2
ROWS = 144
SUM_ROWS = 136
EXTRA = 128
AXES = ("y", "zl", "x", "zh", "c")
CHIPS = ("zh", "y", "zl", "x")
DP = ("y", "zl", "x")
MOST = 149000.0
PARAMS = pltpu.CompilerParams(vmem_limit_bytes=50 * 1024 * 1024)
COST = pl.CostEstimate(flops=1, transcendentals=0, bytes_accessed=1)
f32, bf16, f16 = jnp.float32, jnp.bfloat16, jnp.float16


def pairs(mask, core=0):
    out = []
    for dev in range(128):
        chip = ((dev >> 1) & 1) * 32 + (dev >> 2)
        to = chip ^ mask
        out.append((dev, ((to & 31) << 2) + ((to >> 5) << 1) + ((dev & 1) ^ core)))
    return out


def swap(block, mask, core=0):
    return lax.ppermute(block, AXES, pairs(mask, core))


def adam_step(parameter, gradient, first_moment, second_moment, step_rate):
    first_moment = beta_first * first_moment + (1.0 - beta_first) * gradient
    second_moment = beta_second * second_moment + (1.0 - beta_second) * gradient * gradient
    update = first_moment / fix_first / (jnp.sqrt(second_moment / fix_second) + adam_eps)
    return (
        (parameter.astype(f32) - step_rate * update).astype(bf16),
        first_moment,
        second_moment,
    )


def fold(values):
    total = values[:, :128]
    for at in range(128, values.shape[1], 128):
        total = total + values[:, at : at + 128]
    return total


def inv_rms(hid):
    squares = jnp.zeros((hid.shape[0], 128), f32)
    for at in range(0, D, BLK):
        wide = hid[:, at : at + BLK].astype(f32)
        squares = squares + fold(wide * wide)
    mean = jnp.sum(squares, axis=1, keepdims=True) * (1.0 / D)
    return lax.rsqrt(mean + norm_eps)


def scale_kernel(core, hid, grad, out, theirs):
    most = jnp.max(jnp.abs(grad[...].astype(f32)), keepdims=True)
    lanes = lax.broadcasted_iota(jnp.int32, out.shape, 1)
    for half in range(2):
        start = pl.multiple_of((half * 2 + 1 - core[0]) * 1024, 1024)
        theirs[:, half * 1024 : half * 1024 + 1024] = hid[:, pl.ds(start, 1024)]
    out[...] = jnp.where(lanes < 64, inv_rms(hid), most)


def next_kernel(hid, out):
    out[...] = jnp.broadcast_to(inv_rms(hid), out.shape)


def products(hid, gain, grad, weight, inv):
    unit = hid[...].astype(f32) * inv[:, :1]
    normed = (unit * gain[...].astype(f32)).astype(bf16)
    part = lax.dot_general(
        normed, grad[...], (((0,), (0,)), ((), ())), preferred_element_type=f32
    )
    back = lax.dot_general(
        grad[...], weight[...], (((1,), (1,)), ((), ())), preferred_element_type=f32
    )
    return part, jnp.sum(back * unit, axis=0, keepdims=True)


def chip_kernel(core, hid, got_hid, gain, grad, got_grad, weight, inv, got_inv, out, after):
    after[...] = jnp.zeros_like(after)
    part, gain_part = products(hid, gain, grad, weight, inv)
    got_part, got_gain = products(got_hid, gain, got_grad, weight, got_inv)
    most = jnp.maximum(
        jnp.max(inv[:, 64:], keepdims=True), jnp.max(got_inv[:, 64:], keepdims=True)
    )
    power = jnp.floor(jnp.log(30000.0 / MOST / jnp.maximum(most, 1e-30)) * 1.4426950408889634)
    scale = jnp.exp(power * 0.6931471805599453)
    part = (part + got_part) * scale
    left = (gain_part + got_gain) * (scale * (1.0 / 64.0))
    pieces = []
    for step in (1.0, 256.0, 65536.0):
        rounded = left.astype(bf16).astype(f32)
        pieces.append(rounded * step)
        left = left - rounded
    for j in range(BLK // 32):
        for b in range(4):
            out[j, b * 32 : b * 32 + 32, :] = part[j * 32 : j * 32 + 32, b * 128 : b * 128 + 128]
        lanes = slice((j // 4) * 128, (j // 4) * 128 + 128)
        rows = [piece[:, lanes] for piece in pieces] + [jnp.broadcast_to(power, (1, 128))]
        rows.append(jnp.zeros((SUM_ROWS - EXTRA - 4, 128), f32))
        out[j, EXTRA:, :] = jnp.concatenate(rows)


def value_step(blocks, hid, inv, weight, gain_out):
    lanes = []
    for j in range(BLK // 32):
        for b in range(4):
            weight[j * 32 : j * 32 + 32, b * 128 : b * 128 + 128] = blocks[
                j, b * 32 : b * 32 + 32, :
            ]
    for j in range(0, BLK // 32, 4):
        rows = [blocks[j + k, EXTRA : EXTRA + 16, :].astype(f32)[:1] for k in range(4)]
        lanes.append((rows[0] + rows[1]) + (rows[2] + rows[3]))
    gain = jnp.concatenate(lanes, axis=1)
    gain_out[...] = gain
    unit = hid[...].astype(f32) * inv[:, :1]
    normed = (unit * gain).astype(bf16)
    return jnp.dot(normed, weight[...], preferred_element_type=f32)


def first_kernel(core, blocks, hid, inv, weight, gain, out):
    part = value_step(blocks, hid, inv, weight, gain)

    @pl.when(pl.program_id(0) == 0)
    def _():
        out[...] = part

    @pl.when(pl.program_id(0) > 0)
    def _():
        out[...] += part


def last_kernel(core, blocks, hid, inv, acc, started, gain_started, weight, gain, out, total):
    part = value_step(blocks, hid, inv, weight, gain)

    @pl.when(pl.program_id(0) == 0)
    def _():
        total[...] = acc[...] + part

    @pl.when(pl.program_id(0) > 0)
    def _():
        total[...] += part

    @pl.when(pl.program_id(0) == pl.num_programs(0) - 1)
    def _():
        out[...] = total[...].astype(bf16)


def shape(dims, dtype):
    return jax.ShapeDtypeStruct(dims, dtype)


def whole(dims):
    return pl.BlockSpec(dims, lambda i, *_: (0,) * len(dims))


def column(i, core):
    return ((i // 2) * 2 + core[0]) * 2 + i % 2


def call(kernel, grid, ins, outs, out_shape, scratch=(), prefetch=1, **more):
    return pl.pallas_call(
        kernel,
        grid_spec=pltpu.PrefetchScalarGridSpec(
            num_scalar_prefetch=prefetch,
            grid=(grid,),
            in_specs=ins,
            out_specs=outs,
            scratch_shapes=scratch,
        ),
        out_shape=out_shape,
        compiler_params=PARAMS,
        cost_estimate=COST,
        **more,
    )


def blocked(rows):
    return rows.reshape(32, 4, 128).transpose(1, 0, 2).reshape(128, 128)


def body(
    hidden_in,
    value_grad,
    value_weight,
    norm_gain,
    owner_map,
    mat_first,
    mat_second,
    vec_first,
    vec_second,
    next_hidden,
):
    y, zl, x = lax.axis_index("y"), lax.axis_index("zl"), lax.axis_index("x")
    zh, core = lax.axis_index("zh"), lax.axis_index("c")
    place = y * 8 + zl * 4 + x
    rep = zh * 2 + core
    owner_weight, owner_gain = owner_map[0], owner_map[1]
    holds_weight = place == owner_weight
    holds_gain = place == owner_gain
    core_at, other_at = core.reshape(1), (1 - core).reshape(1)
    gain_row = norm_gain.reshape(1, D)

    hid_spec = pl.BlockSpec((TOK, BLK), lambda i, core: (0, column(i, core)))
    inv, theirs = call(
        scale_kernel,
        3,
        [
            pl.BlockSpec((256, D), lambda i, core: (i, 0)),
            pl.BlockSpec((256, KV), lambda i, core: (i, 0)),
        ],
        (
            pl.BlockSpec((256, 128), lambda i, core: (i, 0)),
            pl.BlockSpec((256, HALF), lambda i, core: (i, 0)),
        ),
        (shape((TOK, 128), f32), shape((TOK, HALF), bf16)),
    )(core_at, hidden_in, value_grad)
    got_hid, got_grad, got_inv = swap(theirs, 0, 1), swap(value_grad, 0, 1), swap(inv, 0, 1)

    owners = (owner_weight, owner_gain)

    def share(picks, at, sources, unit, tie):
        kept = picks[0]
        is_mat = jnp.arange(kept.shape[0])[:, None] < kept.shape[0] - 2
        for k in range(1, len(picks)):
            got = swap(picks[k], k * unit)
            mine = jnp.where(is_mat, (at ^ k) == sources[0], (at ^ k) == sources[1])
            kept = jnp.where(mine, got, kept)
        return kept + tie

    def first_pick(k):
        mats = [
            lax.dynamic_slice_in_dim(m[0], (y ^ k) * 256, 256).astype(f16)
            for m in (mat_first, mat_second)
        ]
        vecs = jnp.concatenate(
            [lax.dynamic_slice_in_dim(v, (y ^ k) * 256, 256, 1) for v in (vec_first, vec_second)],
            axis=1,
        )
        high = lax.reduce_precision(vecs, 5, 10)
        return jnp.concatenate(
            mats + [high.astype(f16), ((vecs - high) * 2048.0).astype(f16)]
        )

    first_picks = [first_pick(k) for k in range(4)]

    side = pl.BlockSpec((1, BLK), lambda i, core: (0, column(i, core)))
    wide = pl.BlockSpec((BLK, KV), lambda i, core: (column(i, core), 0))
    scaled, after = call(
        chip_kernel,
        4,
        [
            hid_spec,
            pl.BlockSpec((TOK, BLK), lambda i, core: (0, i)),
            side,
            whole((TOK, KV)),
            whole((TOK, KV)),
            wide,
            whole((TOK, 128)),
            whole((TOK, 128)),
        ],
        (pl.BlockSpec((16, SUM_ROWS, 128), lambda i, core: (i, 0, 0)), whole((1, KV))),
        (shape((64, SUM_ROWS, 128), f32), shape((1, KV), f32)),
    )(core_at, hidden_in, got_hid, gain_row, value_grad, got_grad, value_weight, inv, got_inv)
    after = after.astype(f16)
    moments = share(first_picks, y, [o >> 3 for o in owners], 8, after)
    next_inv = pl.pallas_call(
        next_kernel,
        grid=(3,),
        in_specs=[pl.BlockSpec((256, D), lambda i: (i, 0))],
        out_specs=pl.BlockSpec((256, 128), lambda i: (i, 0)),
        out_shape=shape((TOK, 128), f32),
        compiler_params=PARAMS,
        cost_estimate=COST,
    )(lax.optimization_barrier((next_hidden, moments))[0])
    rows = moments[:-2].reshape(2, 8, 32, KV)

    def last_pick(k):
        got = lax.dynamic_index_in_dim(rows, (zl * 4 + x) ^ k, 1, keepdims=False)
        return jnp.concatenate([got.reshape(64, KV), moments[-2:]])

    last_picks = [last_pick(k) for k in range(8)]
    moments = share(last_picks, zl * 4 + x, [o & 7 for o in owners], 1, jnp.zeros((), f16))
    moments = moments.astype(f32)
    old_mats = moments[:64]
    old_vecs = lax.dynamic_slice_in_dim(
        moments[64:].reshape(2, 2, 256), (zl * 4 + x) * 32, 32, axis=2
    )
    old_vecs = old_vecs[0] + old_vecs[1] * (1.0 / 2048.0)

    parts = lax.all_to_all(scaled.astype(f16), CHIPS, 0, 0, tiled=True)
    power = parts[:, EXTRA + 3, :1].astype(f32)
    grad_rows = jnp.sum(parts[:, :EXTRA].astype(f32) * jnp.exp2(-power)[:, :, None], axis=0)
    terms = [parts[:, EXTRA + k].astype(f32) * (64.0 / 256.0**k) for k in range(3)]
    lanes = jnp.sum((terms[0] + terms[1] + terms[2]) * jnp.exp2(-power), axis=0)
    first_row = rep * 1024 + place * 32
    own_lanes = (jnp.arange(128) >> 5) == x
    grad_gain = lax.dynamic_slice_in_dim(lanes, x * 32, 32)

    own_rows = blocked(lax.dynamic_slice_in_dim(value_weight, first_row, 32))
    weight_rows = adam_step(
        own_rows, grad_rows, blocked(old_mats[:32]), blocked(old_mats[32:]), learn_rate
    )[0]
    gain_part = lax.dynamic_slice_in_dim(norm_gain, first_row, 32)
    gain_new = adam_step(gain_part, grad_gain, old_vecs[0], old_vecs[1], gain_rate)[0]
    gain_lanes = jnp.where(own_lanes, jnp.tile(gain_new, 4), jnp.zeros((), bf16))
    weight_rows = weight_rows + (next_inv[0, 0] * 0.0).astype(bf16)
    block = jnp.concatenate(
        [weight_rows, gain_lanes[None], jnp.zeros((ROWS - EXTRA - 1, 128), bf16)]
    )
    own = lax.all_to_all(
        jnp.broadcast_to(block[None], (64, ROWS, 128)), CHIPS, 0, 0, tiled=True
    )
    other = swap(own, 0, 1)

    lanes = jnp.where(own_lanes, lanes, 0.0)
    high = lax.reduce_precision(lanes, 8, 10)
    most = jnp.max(jnp.maximum(jnp.abs(grad_rows), jnp.abs(lanes)[None] * (1.0 / 64.0)))
    power = jnp.floor(jnp.log2(16384.0 / jnp.maximum(most, 1e-30)))
    scale = jnp.exp2(power)
    rows = [
        high * (scale * (1.0 / 64.0)),
        (lanes - high) * (scale * 32.0),
        jnp.full((256,), power),
    ]
    natural = (grad_rows * scale).reshape(4, 32, 128).transpose(1, 0, 2).reshape(32, KV)
    sent = jnp.concatenate([natural, jnp.concatenate(rows)[None]]).astype(f16)
    grads = lax.all_to_all(jnp.broadcast_to(sent[None], (32, 33, KV)), DP, 0, 0, tiled=True)

    value_ins = [
        pl.BlockSpec((16, ROWS, 128), lambda i, core: (i, 0, 0)),
        pl.BlockSpec((TOK, BLK), lambda i, core: (0, column(i, core))),
        whole((TOK, 128)),
    ]
    gain_spec = pl.BlockSpec((1, BLK), lambda i, core: (0, column(i, core)))
    any_spec = pl.BlockSpec(memory_space=pl.ANY)
    started, gain_started, acc = call(
        first_kernel,
        4,
        value_ins,
        (wide, gain_spec, whole((TOK, KV))),
        (shape((D, KV), bf16), shape((1, D), f32), shape((TOK, KV), f32)),
    )(core_at, own, next_hidden, next_inv)
    new_weight, new_gain, next_values = call(
        last_kernel,
        4,
        value_ins + [whole((TOK, KV)), any_spec, any_spec],
        (wide, gain_spec, whole((TOK, KV))),
        (shape((D, KV), bf16), shape((1, D), f32), shape((TOK, KV), bf16)),
        [pltpu.VMEM((TOK, KV), f32)],
        input_output_aliases={5: 0, 6: 1},
    )(other_at, other, next_hidden, next_inv, acc, started, gain_started)
    new_gain = new_gain.reshape(D).astype(bf16)

    grads, _ = lax.optimization_barrier((grads, next_values))
    ends = grads[:, 32].astype(f32)
    back = jnp.exp2(-ends[:, 256:384])
    gain_sums = (ends[:, :128] * 64.0 + ends[:, 128:256] * (1.0 / 32.0)) * back
    rep_gain = jnp.sum(gain_sums.reshape(8, 4, 128), axis=1).reshape(1, 1024)
    first_vec = beta_first * vec_first + (1.0 - beta_first) * rep_gain
    second_vec = beta_second * vec_second + (1.0 - beta_second) * rep_gain * rep_gain
    new_vec_first = jnp.where(holds_gain, first_vec, vec_first)
    new_vec_second = jnp.where(holds_gain, second_vec, vec_second)
    rep_rows = grads[:, :32].astype(f32) * back[:, :1, None]
    old_first, old_second = mat_first.reshape(32, 32, KV), mat_second.reshape(32, 32, KV)
    first_mat = beta_first * old_first + (1.0 - beta_first) * rep_rows
    second_mat = beta_second * old_second + (1.0 - beta_second) * rep_rows * rep_rows
    new_mat_first = jnp.where(holds_weight, first_mat, old_first).reshape(1, 1024, KV)
    new_mat_second = jnp.where(holds_weight, second_mat, old_second).reshape(1, 1024, KV)
    return (
        new_weight,
        new_gain,
        new_mat_first,
        new_mat_second,
        new_vec_first,
        new_vec_second,
        next_values,
    )


def solution(mesh):
    fine = Mesh(mesh.devices.reshape(4, 2, 4, 2, 2), AXES)
    rep = ("zh", "c")
    tokens = P(AXES, None)
    return jax.shard_map(
        body,
        mesh=fine,
        in_specs=(
            tokens,
            tokens,
            P(),
            P(),
            P(),
            P(DP, rep, None),
            P(DP, rep, None),
            P(DP, rep),
            P(DP, rep),
            tokens,
        ),
        out_specs=(
            P(),
            P(),
            P(DP, rep, None),
            P(DP, rep, None),
            P(DP, rep),
            P(DP, rep),
            tokens,
        ),
        check_vma=False,
    )
```

```python
import jax
import jax.numpy as jnp
from jax import lax
from jax.experimental import pallas as pl
from jax.experimental.pallas import tpu as pltpu
from jax.sharding import Mesh, PartitionSpec as P

norm_eps = 1e-05
adam_eps = 1e-08
beta_first = 0.9
beta_second = 0.95
learn_rate = 0.001
gain_rate = 0.02
fix_first = 1.0 - 0.9**10
fix_second = 1.0 - 0.95**10

D, KV, TOK = 4096, 512, 768
BLK = 512
HALF = D // 2
ROWS = 144
SUM_ROWS = 136
EXTRA = 128
AXES = ("y", "zl", "x", "zh", "c")
CHIPS = ("zh", "y", "zl", "x")
DP = ("y", "zl", "x")
MOST = 149000.0
PARAMS = pltpu.CompilerParams(vmem_limit_bytes=50 * 1024 * 1024)
COST = pl.CostEstimate(flops=1, transcendentals=0, bytes_accessed=1)
f32, bf16, f16 = jnp.float32, jnp.bfloat16, jnp.float16


def pairs(mask, core=0):
    out = []
    for dev in range(128):
        chip = ((dev >> 1) & 1) * 32 + (dev >> 2)
        to = chip ^ mask
        out.append((dev, ((to & 31) << 2) + ((to >> 5) << 1) + ((dev & 1) ^ core)))
    return out


def swap(block, mask, core=0):
    return lax.ppermute(block, AXES, pairs(mask, core))


def adam_step(parameter, gradient, first_moment, second_moment, step_rate):
    first_moment = beta_first * first_moment + (1.0 - beta_first) * gradient
    second_moment = beta_second * second_moment + (1.0 - beta_second) * gradient * gradient
    update = first_moment / fix_first / (jnp.sqrt(second_moment / fix_second) + adam_eps)
    return (
        (parameter.astype(f32) - step_rate * update).astype(bf16),
        first_moment,
        second_moment,
    )


def fold(values):
    total = values[:, :128]
    for at in range(128, values.shape[1], 128):
        total = total + values[:, at : at + 128]
    return total


def inv_rms(hid):
    squares = jnp.zeros((hid.shape[0], 128), f32)
    for at in range(0, D, BLK):
        wide = hid[:, at : at + BLK].astype(f32)
        squares = squares + fold(wide * wide)
    mean = jnp.sum(squares, axis=1, keepdims=True) * (1.0 / D)
    return lax.rsqrt(mean + norm_eps)


def scale_kernel(core, hid, grad, out, theirs):
    most = jnp.max(jnp.abs(grad[...].astype(f32)), keepdims=True)
    lanes = lax.broadcasted_iota(jnp.int32, out.shape, 1)
    for half in range(2):
        start = pl.multiple_of((half * 2 + 1 - core[0]) * 1024, 1024)
        theirs[:, half * 1024 : half * 1024 + 1024] = hid[:, pl.ds(start, 1024)]
    out[...] = jnp.where(lanes < 64, inv_rms(hid), most)


def next_kernel(hid, out):
    out[...] = jnp.broadcast_to(inv_rms(hid), out.shape)


def products(hid, gain, grad, weight, inv):
    unit = hid[...].astype(f32) * inv[:, :1]
    normed = (unit * gain[...].astype(f32)).astype(bf16)
    part = lax.dot_general(
        normed, grad[...], (((0,), (0,)), ((), ())), preferred_element_type=f32
    )
    back = lax.dot_general(
        grad[...], weight[...], (((1,), (1,)), ((), ())), preferred_element_type=f32
    )
    return part, jnp.sum(back * unit, axis=0, keepdims=True)


def chip_kernel(core, hid, got_hid, gain, grad, got_grad, weight, inv, got_inv, firsts, seconds, out, after):
    after[...] = jnp.zeros_like(after)
    part, gain_part = products(hid, gain, grad, weight, inv)
    got_part, got_gain = products(got_hid, gain, got_grad, weight, got_inv)
    most = jnp.maximum(
        jnp.max(inv[:, 64:], keepdims=True), jnp.max(got_inv[:, 64:], keepdims=True)
    )
    power = jnp.floor(jnp.log(30000.0 / MOST / jnp.maximum(most, 1e-30)) * 1.4426950408889634)
    scale = jnp.exp(power * 0.6931471805599453)
    part = (part + got_part) * scale
    left = (gain_part + got_gain) * (scale * (1.0 / 64.0))
    pieces = []
    for step in (1.0, 256.0, 65536.0):
        rounded = left.astype(bf16).astype(f32)
        pieces.append(rounded * step)
        left = left - rounded
    vecs = []
    for vec in (firsts, seconds):
        whole_part = vec[...] * 4096.0
        rounded = whole_part.astype(bf16).astype(f32)
        vecs += [rounded, (whole_part - rounded) * 256.0]
    for j in range(BLK // 32):
        for b in range(4):
            out[j, b * 32 : b * 32 + 32, :] = part[j * 32 : j * 32 + 32, b * 128 : b * 128 + 128]
        lanes = slice((j // 4) * 128, (j // 4) * 128 + 128)
        rows = [piece[:, lanes] for piece in pieces] + [jnp.broadcast_to(power, (1, 128))]
        rows += [vec[:, lanes] for vec in vecs]
        out[j, EXTRA:, :] = jnp.concatenate(rows)


def value_step(blocks, hid, inv, weight, gain_out):
    lanes = []
    for j in range(BLK // 32):
        for b in range(4):
            weight[j * 32 : j * 32 + 32, b * 128 : b * 128 + 128] = blocks[
                j, b * 32 : b * 32 + 32, :
            ]
    for j in range(0, BLK // 32, 4):
        rows = [blocks[j + k, EXTRA : EXTRA + 16, :].astype(f32)[:1] for k in range(4)]
        lanes.append((rows[0] + rows[1]) + (rows[2] + rows[3]))
    gain = jnp.concatenate(lanes, axis=1)
    gain_out[...] = gain
    unit = hid[...].astype(f32) * inv[:, :1]
    normed = (unit * gain).astype(bf16)
    return jnp.dot(normed, weight[...], preferred_element_type=f32)


def first_kernel(core, blocks, hid, inv, weight, gain, out):
    part = value_step(blocks, hid, inv, weight, gain)

    @pl.when(pl.program_id(0) == 0)
    def _():
        out[...] = part

    @pl.when(pl.program_id(0) > 0)
    def _():
        out[...] += part


def last_kernel(core, blocks, hid, inv, acc, started, gain_started, weight, gain, out, total):
    part = value_step(blocks, hid, inv, weight, gain)

    @pl.when(pl.program_id(0) == 0)
    def _():
        total[...] = acc[...] + part

    @pl.when(pl.program_id(0) > 0)
    def _():
        total[...] += part

    @pl.when(pl.program_id(0) == pl.num_programs(0) - 1)
    def _():
        out[...] = total[...].astype(bf16)


def shape(dims, dtype):
    return jax.ShapeDtypeStruct(dims, dtype)


def whole(dims):
    return pl.BlockSpec(dims, lambda i, *_: (0,) * len(dims))


def column(i, core):
    return ((i // 2) * 2 + core[0]) * 2 + i % 2


def call(kernel, grid, ins, outs, out_shape, scratch=(), prefetch=1, **more):
    return pl.pallas_call(
        kernel,
        grid_spec=pltpu.PrefetchScalarGridSpec(
            num_scalar_prefetch=prefetch,
            grid=(grid,),
            in_specs=ins,
            out_specs=outs,
            scratch_shapes=scratch,
        ),
        out_shape=out_shape,
        compiler_params=PARAMS,
        cost_estimate=COST,
        **more,
    )


def blocked(rows):
    return rows.reshape(32, 4, 128).transpose(1, 0, 2).reshape(128, 128)


def body(
    hidden_in,
    value_grad,
    value_weight,
    norm_gain,
    owner_map,
    mat_first,
    mat_second,
    vec_first,
    vec_second,
    next_hidden,
):
    y, zl, x = lax.axis_index("y"), lax.axis_index("zl"), lax.axis_index("x")
    zh, core = lax.axis_index("zh"), lax.axis_index("c")
    place = y * 8 + zl * 4 + x
    rep = zh * 2 + core
    owner_weight, owner_gain = owner_map[0], owner_map[1]
    holds_weight = place == owner_weight
    holds_gain = place == owner_gain
    core_at, other_at = core.reshape(1), (1 - core).reshape(1)
    gain_row = norm_gain.reshape(1, D)

    hid_spec = pl.BlockSpec((TOK, BLK), lambda i, core: (0, column(i, core)))
    inv, theirs = call(
        scale_kernel,
        2,
        [
            pl.BlockSpec((384, D), lambda i, core: (i, 0)),
            pl.BlockSpec((384, KV), lambda i, core: (i, 0)),
        ],
        (
            pl.BlockSpec((384, 128), lambda i, core: (i, 0)),
            pl.BlockSpec((384, HALF), lambda i, core: (i, 0)),
        ),
        (shape((TOK, 128), f32), shape((TOK, HALF), bf16)),
    )(core_at, hidden_in, value_grad)
    got_hid, got_grad, got_inv = swap(theirs, 0, 1), swap(value_grad, 0, 1), swap(inv, 0, 1)

    def share(picks, at, source, unit):
        kept = picks[0]
        for k in range(1, len(picks)):
            kept = jnp.where((at ^ k) == source, swap(picks[k], k * unit), kept)
        return kept

    def first_pick(k):
        return jnp.concatenate(
            [
                lax.dynamic_slice_in_dim(m[0], (y ^ k) * 256, 256).astype(f16)
                for m in (mat_first, mat_second)
            ]
        )

    first_picks = [first_pick(k) for k in range(4)]

    side = pl.BlockSpec((1, BLK), lambda i, core: (0, column(i, core)))
    wide = pl.BlockSpec((BLK, KV), lambda i, core: (column(i, core), 0))
    scaled, after = call(
        chip_kernel,
        4,
        [
            hid_spec,
            pl.BlockSpec((TOK, BLK), lambda i, core: (0, i)),
            side,
            whole((TOK, KV)),
            whole((TOK, KV)),
            wide,
            whole((TOK, 128)),
            whole((TOK, 128)),
            pl.BlockSpec((1, BLK), lambda i, core: (0, i % 2)),
            pl.BlockSpec((1, BLK), lambda i, core: (0, i % 2)),
        ],
        (pl.BlockSpec((16, SUM_ROWS, 128), lambda i, core: (i, 0, 0)), whole((1, KV))),
        (shape((64, SUM_ROWS, 128), f32), shape((1, KV), f32)),
    )(
        core_at,
        hidden_in,
        got_hid,
        gain_row,
        value_grad,
        got_grad,
        value_weight,
        inv,
        got_inv,
        vec_first,
        vec_second,
    )
    moments = share(first_picks, y, owner_weight >> 3, 8) + after.astype(f16)
    next_inv = pl.pallas_call(
        next_kernel,
        grid=(3,),
        in_specs=[pl.BlockSpec((256, D), lambda i: (i, 0))],
        out_specs=pl.BlockSpec((256, 128), lambda i: (i, 0)),
        out_shape=shape((TOK, 128), f32),
        compiler_params=PARAMS,
        cost_estimate=pl.CostEstimate(flops=17 * 10**9, transcendentals=0, bytes_accessed=1),
    )(lax.optimization_barrier((next_hidden, moments))[0])
    moments, next_inv = lax.optimization_barrier((moments, next_inv))
    moments = moments.reshape(2, 8, 32, KV)
    last_picks = [
        lax.dynamic_index_in_dim(moments, (zl * 4 + x) ^ k, 1, keepdims=False).reshape(64, KV)
        for k in range(8)
    ]
    arrived = [swap(last_picks[k], k) for k in range(1, 8)]

    parts = lax.all_to_all(scaled.astype(f16), CHIPS, 0, 0, tiled=True)
    parts, early = lax.optimization_barrier((parts, arrived[:5]))
    arrived = early + arrived[5:]
    back = jnp.exp2(-parts[:, EXTRA + 3, :1].astype(f32))
    summed = jnp.sum(parts.astype(f32) * back[:, :, None], axis=0)
    grad_rows = summed[:EXTRA]
    lanes = summed[EXTRA] * 64.0 + summed[EXTRA + 1] * (64.0 / 256.0)
    lanes = lanes + summed[EXTRA + 2] * (64.0 / 65536.0)
    own_lanes = (jnp.arange(128) >> 5) == x
    lanes = jnp.where(own_lanes, lanes, 0.0)
    high = lax.reduce_precision(lanes, 8, 10)
    most = jnp.maximum(jnp.max(jnp.abs(grad_rows), axis=0), jnp.abs(lanes) * (1.0 / 64.0))
    power = jnp.floor(jnp.log2(16384.0 / jnp.maximum(most, 1e-30)))
    scale = jnp.exp2(power)
    gain_row = [high * (scale * (1.0 / 64.0)), (lanes - high) * (scale * 32.0)]
    gain_row = jnp.concatenate(gain_row + [jnp.zeros((256,), f32)])
    natural = (grad_rows * scale).reshape(4, 32, 128).transpose(1, 0, 2).reshape(32, KV)
    sent = jnp.concatenate([natural, gain_row[None], jnp.tile(power, 4)[None]]).astype(f16)
    sent = jnp.broadcast_to(sent[None], (32, 34, KV))
    old_vecs = lax.dynamic_index_in_dim(parts, zh * 32 + owner_gain, 0, keepdims=False)
    old_vecs = old_vecs[EXTRA + 4 :].astype(f32) * (1.0 / 4096.0)
    old_vecs = lax.dynamic_slice_in_dim(old_vecs, x * 32, 32, 1)
    old_vecs = old_vecs[0::2] + old_vecs[1::2] * (1.0 / 256.0)
    first_row = rep * 1024 + place * 32
    grad_gain = lax.dynamic_slice_in_dim(lanes, x * 32, 32)

    gain_part = lax.dynamic_slice_in_dim(norm_gain, first_row, 32)
    gain_new = adam_step(gain_part, grad_gain, old_vecs[0], old_vecs[1], gain_rate)[0]
    gain_lanes = jnp.where(own_lanes, jnp.tile(gain_new, 4), jnp.zeros((), bf16))
    arrived, grad_rows, sent, gain_lanes = lax.optimization_barrier(
        (arrived, grad_rows, sent, gain_lanes)
    )
    old_mats = last_picks[0]
    for k in range(1, 8):
        source = (zl * 4 + x) ^ k == (owner_weight & 7)
        old_mats = jnp.where(source, arrived[k - 1], old_mats)
    old_mats = old_mats.astype(f32)

    own_rows = blocked(lax.dynamic_slice_in_dim(value_weight, first_row, 32))
    weight_rows = adam_step(
        own_rows, grad_rows, blocked(old_mats[:32]), blocked(old_mats[32:]), learn_rate
    )[0]
    block = jnp.concatenate(
        [weight_rows, gain_lanes[None], jnp.zeros((ROWS - EXTRA - 1, 128), bf16)]
    )

    own = lax.all_to_all(
        jnp.broadcast_to(block[None], (64, ROWS, 128)), CHIPS, 0, 0, tiled=True
    )
    other = swap(own, 0, 1)
    grads = lax.all_to_all(sent, DP, 0, 0, tiled=True)

    value_ins = [
        pl.BlockSpec((16, ROWS, 128), lambda i, core: (i, 0, 0)),
        pl.BlockSpec((TOK, BLK), lambda i, core: (0, column(i, core))),
        whole((TOK, 128)),
    ]
    gain_spec = pl.BlockSpec((1, BLK), lambda i, core: (0, column(i, core)))
    any_spec = pl.BlockSpec(memory_space=pl.ANY)
    started, gain_started, acc = call(
        first_kernel,
        4,
        value_ins,
        (wide, gain_spec, whole((TOK, KV))),
        (shape((D, KV), bf16), shape((1, D), f32), shape((TOK, KV), f32)),
    )(core_at, own, next_hidden, next_inv)
    new_weight, new_gain, next_values = call(
        last_kernel,
        4,
        value_ins + [whole((TOK, KV)), any_spec, any_spec],
        (wide, gain_spec, whole((TOK, KV))),
        (shape((D, KV), bf16), shape((1, D), f32), shape((TOK, KV), bf16)),
        [pltpu.VMEM((TOK, KV), f32)],
        input_output_aliases={5: 0, 6: 1},
    )(other_at, other, next_hidden, next_inv, acc, started, gain_started)
    new_gain = new_gain.reshape(D).astype(bf16)

    grads, _ = lax.optimization_barrier((grads, next_values))
    ends, back = grads[:, 32].astype(f32), jnp.exp2(-grads[:, 33].astype(f32))
    gain_sums = (ends[:, :128] * 64.0 + ends[:, 128:256] * (1.0 / 32.0)) * back[:, :128]
    rep_gain = jnp.sum(gain_sums.reshape(8, 4, 128), axis=1).reshape(1, 1024)
    first_vec = beta_first * vec_first + (1.0 - beta_first) * rep_gain
    second_vec = beta_second * vec_second + (1.0 - beta_second) * rep_gain * rep_gain
    new_vec_first = jnp.where(holds_gain, first_vec, vec_first)
    new_vec_second = jnp.where(holds_gain, second_vec, vec_second)
    rep_rows = grads[:, :32].astype(f32) * back[:, None]
    old_first, old_second = mat_first.reshape(32, 32, KV), mat_second.reshape(32, 32, KV)
    first_mat = beta_first * old_first + (1.0 - beta_first) * rep_rows
    second_mat = beta_second * old_second + (1.0 - beta_second) * rep_rows * rep_rows
    new_mat_first = jnp.where(holds_weight, first_mat, old_first).reshape(1, 1024, KV)
    new_mat_second = jnp.where(holds_weight, second_mat, old_second).reshape(1, 1024, KV)
    return (
        new_weight,
        new_gain,
        new_mat_first,
        new_mat_second,
        new_vec_first,
        new_vec_second,
        next_values,
    )


def solution(mesh):
    fine = Mesh(mesh.devices.reshape(4, 2, 4, 2, 2), AXES)
    rep = ("zh", "c")
    tokens = P(AXES, None)
    return jax.shard_map(
        body,
        mesh=fine,
        in_specs=(
            tokens,
            tokens,
            P(),
            P(),
            P(),
            P(DP, rep, None),
            P(DP, rep, None),
            P(DP, rep),
            P(DP, rep),
            tokens,
        ),
        out_specs=(
            P(),
            P(),
            P(DP, rep, None),
            P(DP, rep, None),
            P(DP, rep),
            P(DP, rep),
            tokens,
        ),
        check_vma=False,
    )
```

```python
import jax
import jax.numpy as jnp
from jax import lax
from jax.experimental import pallas as pl
from jax.experimental.pallas import tpu as pltpu
from jax.sharding import Mesh, PartitionSpec as P

norm_eps = 1e-05
adam_eps = 1e-08
beta_first = 0.9
beta_second = 0.95
learn_rate = 0.001
gain_rate = 0.02
fix_first = 1.0 - 0.9**10
fix_second = 1.0 - 0.95**10

D, KV, TOK = 4096, 512, 768
BLK = 512
HALF = D // 2
ROWS = 144
SUM_ROWS = 136
EXTRA = 128
AXES = ("y", "zl", "x", "zh", "c")
CHIPS = ("zh", "y", "zl", "x")
DP = ("y", "zl", "x")
MOST = 149000.0
PARAMS = pltpu.CompilerParams(vmem_limit_bytes=50 * 1024 * 1024)
COST = pl.CostEstimate(flops=1, transcendentals=0, bytes_accessed=1)
f32, bf16, f16 = jnp.float32, jnp.bfloat16, jnp.float16


def pairs(mask, core=0):
    out = []
    for dev in range(128):
        chip = ((dev >> 1) & 1) * 32 + (dev >> 2)
        to = chip ^ mask
        out.append((dev, ((to & 31) << 2) + ((to >> 5) << 1) + ((dev & 1) ^ core)))
    return out


def swap(block, mask, core=0):
    return lax.ppermute(block, AXES, pairs(mask, core))


def adam_step(parameter, gradient, first_moment, second_moment, step_rate):
    first_moment = beta_first * first_moment + (1.0 - beta_first) * gradient
    second_moment = beta_second * second_moment + (1.0 - beta_second) * gradient * gradient
    update = first_moment / fix_first / (jnp.sqrt(second_moment / fix_second) + adam_eps)
    return (
        (parameter.astype(f32) - step_rate * update).astype(bf16),
        first_moment,
        second_moment,
    )


def hbm(x):
    return pltpu.with_memory_space_constraint(x, pltpu.HBM)


def fold(values):
    total = values[:, :128]
    for at in range(128, values.shape[1], 128):
        total = total + values[:, at : at + 128]
    return total


def inv_rms(hid):
    squares = jnp.zeros((hid.shape[0], 128), f32)
    for at in range(0, D, BLK):
        wide = hid[:, at : at + BLK].astype(f32)
        squares = squares + fold(wide * wide)
    mean = jnp.sum(squares, axis=1, keepdims=True) * (1.0 / D)
    return lax.rsqrt(mean + norm_eps)


def scale_kernel(core, hid, grad, out, theirs):
    most = jnp.max(jnp.abs(grad[...].astype(f32)), keepdims=True)
    lanes = lax.broadcasted_iota(jnp.int32, out.shape, 1)
    for half in range(2):
        start = pl.multiple_of((half * 2 + 1 - core[0]) * 1024, 1024)
        theirs[:, half * 1024 : half * 1024 + 1024] = hid[:, pl.ds(start, 1024)]
    out[...] = jnp.where(lanes < 64, inv_rms(hid), most)


def next_kernel(hid, out):
    out[...] = jnp.broadcast_to(inv_rms(hid), out.shape)


def products(hid, gain, grad, weight, inv):
    unit = hid[...].astype(f32) * inv[:, :1]
    normed = (unit * gain[...].astype(f32)).astype(bf16)
    part = lax.dot_general(
        normed, grad[...], (((0,), (0,)), ((), ())), preferred_element_type=f32
    )
    back = lax.dot_general(
        grad[...], weight[...], (((1,), (1,)), ((), ())), preferred_element_type=f32
    )
    return part, jnp.sum(back * unit, axis=0, keepdims=True)


def chip_kernel(core, hid, got_hid, gain, grad, got_grad, weight, inv, got_inv, firsts, seconds, out, after):
    after[...] = jnp.zeros_like(after)
    part, gain_part = products(hid, gain, grad, weight, inv)
    got_part, got_gain = products(got_hid, gain, got_grad, weight, got_inv)
    most = jnp.maximum(
        jnp.max(inv[:, 64:], keepdims=True), jnp.max(got_inv[:, 64:], keepdims=True)
    )
    power = jnp.floor(jnp.log(30000.0 / MOST / jnp.maximum(most, 1e-30)) * 1.4426950408889634)
    scale = jnp.exp(power * 0.6931471805599453)
    part = (part + got_part) * scale
    left = (gain_part + got_gain) * (scale * (1.0 / 64.0))
    pieces = []
    for step in (1.0, 256.0, 65536.0):
        rounded = left.astype(bf16).astype(f32)
        pieces.append(rounded * step)
        left = left - rounded
    vecs = []
    for vec in (firsts, seconds):
        whole_part = vec[...] * 4096.0
        rounded = whole_part.astype(bf16).astype(f32)
        vecs += [rounded, (whole_part - rounded) * 256.0]
    for j in range(BLK // 32):
        for b in range(4):
            out[j, b * 32 : b * 32 + 32, :] = part[j * 32 : j * 32 + 32, b * 128 : b * 128 + 128]
        lanes = slice((j // 4) * 128, (j // 4) * 128 + 128)
        rows = [piece[:, lanes] for piece in pieces] + [jnp.broadcast_to(power, (1, 128))]
        rows += [vec[:, lanes] for vec in vecs]
        out[j, EXTRA:, :] = jnp.concatenate(rows)


def value_step(blocks, hid, inv, weight, gain_out):
    lanes = []
    for j in range(BLK // 32):
        for b in range(4):
            weight[j * 32 : j * 32 + 32, b * 128 : b * 128 + 128] = blocks[
                j, b * 32 : b * 32 + 32, :
            ]
    for j in range(0, BLK // 32, 4):
        rows = [blocks[j + k, EXTRA : EXTRA + 16, :].astype(f32)[:1] for k in range(4)]
        lanes.append((rows[0] + rows[1]) + (rows[2] + rows[3]))
    gain = jnp.concatenate(lanes, axis=1)
    gain_out[...] = gain
    unit = hid[...].astype(f32) * inv[:, :1]
    normed = (unit * gain).astype(bf16)
    return jnp.dot(normed, weight[...], preferred_element_type=f32)


def first_kernel(core, blocks, hid, inv, weight, gain, out):
    part = value_step(blocks, hid, inv, weight, gain)

    @pl.when(pl.program_id(0) == 0)
    def _():
        out[...] = part

    @pl.when(pl.program_id(0) > 0)
    def _():
        out[...] += part


def last_kernel(core, blocks, hid, inv, acc, started, gain_started, weight, gain, out, total):
    part = value_step(blocks, hid, inv, weight, gain)

    @pl.when(pl.program_id(0) == 0)
    def _():
        total[...] = acc[...] + part

    @pl.when(pl.program_id(0) > 0)
    def _():
        total[...] += part

    @pl.when(pl.program_id(0) == pl.num_programs(0) - 1)
    def _():
        out[...] = total[...].astype(bf16)


def shape(dims, dtype):
    return jax.ShapeDtypeStruct(dims, dtype)


def whole(dims):
    return pl.BlockSpec(dims, lambda i, *_: (0,) * len(dims))


def column(i, core):
    return ((i // 2) * 2 + core[0]) * 2 + i % 2


def call(kernel, grid, ins, outs, out_shape, scratch=(), prefetch=1, params=PARAMS, **more):
    return pl.pallas_call(
        kernel,
        grid_spec=pltpu.PrefetchScalarGridSpec(
            num_scalar_prefetch=prefetch,
            grid=(grid,),
            in_specs=ins,
            out_specs=outs,
            scratch_shapes=scratch,
        ),
        out_shape=out_shape,
        compiler_params=params,
        cost_estimate=COST,
        **more,
    )


def blocked(rows):
    return rows.reshape(32, 4, 128).transpose(1, 0, 2).reshape(128, 128)


def body(
    hidden_in,
    value_grad,
    value_weight,
    norm_gain,
    owner_map,
    mat_first,
    mat_second,
    vec_first,
    vec_second,
    next_hidden,
):
    y, zl, x = lax.axis_index("y"), lax.axis_index("zl"), lax.axis_index("x")
    zh, core = lax.axis_index("zh"), lax.axis_index("c")
    place = y * 8 + zl * 4 + x
    rep = zh * 2 + core
    owner_weight, owner_gain = owner_map[0], owner_map[1]
    holds_weight = place == owner_weight
    holds_gain = place == owner_gain
    core_at, other_at = core.reshape(1), (1 - core).reshape(1)
    gain_row = norm_gain.reshape(1, D)

    hid_spec = pl.BlockSpec((TOK, BLK), lambda i, core: (0, column(i, core)))
    inv, theirs = call(
        scale_kernel,
        2,
        [
            pl.BlockSpec((384, D), lambda i, core: (i, 0)),
            pl.BlockSpec((384, KV), lambda i, core: (i, 0)),
        ],
        (
            pl.BlockSpec((384, 128), lambda i, core: (i, 0)),
            pl.BlockSpec((384, HALF), lambda i, core: (i, 0)),
        ),
        (shape((TOK, 128), f32), shape((TOK, HALF), bf16)),
    )(core_at, hidden_in, value_grad)
    got_hid, got_grad, got_inv = swap(theirs, 0, 1), swap(value_grad, 0, 1), swap(inv, 0, 1)

    def share(picks, at, source, unit):
        kept = picks[0]
        for k in range(1, len(picks)):
            kept = jnp.where((at ^ k) == source, swap(picks[k], k * unit), kept)
        return kept

    def first_pick(k):
        return jnp.concatenate(
            [
                lax.dynamic_slice_in_dim(m[0], (y ^ k) * 256, 256).astype(f16)
                for m in (mat_first, mat_second)
            ]
        )

    first_picks = [first_pick(k) for k in range(4)]

    side = pl.BlockSpec((1, BLK), lambda i, core: (0, column(i, core)))
    wide = pl.BlockSpec((BLK, KV), lambda i, core: (column(i, core), 0))
    scaled, after = call(
        chip_kernel,
        4,
        [
            hid_spec,
            pl.BlockSpec((TOK, BLK), lambda i, core: (0, i)),
            side,
            whole((TOK, KV)),
            whole((TOK, KV)),
            wide,
            whole((TOK, 128)),
            whole((TOK, 128)),
            pl.BlockSpec((1, BLK), lambda i, core: (0, i % 2)),
            pl.BlockSpec((1, BLK), lambda i, core: (0, i % 2)),
        ],
        (pl.BlockSpec((16, SUM_ROWS, 128), lambda i, core: (i, 0, 0)), whole((1, KV))),
        (shape((64, SUM_ROWS, 128), f32), shape((1, KV), f32)),
        params=pltpu.CompilerParams(vmem_limit_bytes=40 * 1024 * 1024),
    )(
        core_at,
        hbm(hidden_in),
        hbm(got_hid),
        gain_row,
        hbm(value_grad),
        hbm(got_grad),
        hbm(value_weight),
        hbm(inv),
        hbm(got_inv),
        vec_first,
        vec_second,
    )
    moments = share(first_picks, y, owner_weight >> 3, 8) + after.astype(f16)
    next_inv = pl.pallas_call(
        next_kernel,
        grid=(3,),
        in_specs=[pl.BlockSpec((256, D), lambda i: (i, 0))],
        out_specs=pl.BlockSpec((256, 128), lambda i: (i, 0)),
        out_shape=shape((TOK, 128), f32),
        compiler_params=PARAMS,
        cost_estimate=pl.CostEstimate(flops=17 * 10**9, transcendentals=0, bytes_accessed=1),
    )(lax.optimization_barrier((next_hidden, moments))[0])
    moments, next_inv = lax.optimization_barrier((moments, next_inv))
    moments = moments.reshape(2, 8, 32, KV)
    last_picks = [
        lax.dynamic_index_in_dim(moments, (zl * 4 + x) ^ k, 1, keepdims=False).reshape(64, KV)
        for k in range(8)
    ]
    arrived = [swap(last_picks[k], k) for k in range(1, 8)]

    parts = lax.all_to_all(scaled.astype(f16), CHIPS, 0, 0, tiled=True)
    parts, early = lax.optimization_barrier((parts, arrived[:5]))
    arrived = early + arrived[5:]
    back = jnp.exp2(-parts[:, EXTRA + 3].astype(f32))
    summed = jnp.sum(parts.astype(f32) * back[:, None], axis=0)
    grad_rows = summed[:EXTRA]
    lanes = summed[EXTRA] * 64.0 + summed[EXTRA + 1] * (64.0 / 256.0)
    lanes = lanes + summed[EXTRA + 2] * (64.0 / 65536.0)
    own_lanes = (jnp.arange(128) >> 5) == x
    lanes = jnp.where(own_lanes, lanes, 0.0)
    most = jnp.maximum(jnp.max(jnp.abs(grad_rows), axis=0), 1e-30)
    power = jnp.floor(jnp.log2(16384.0 / most))
    sent = (grad_rows * jnp.exp2(power)).reshape(4, 32, 128).transpose(1, 0, 2)
    sent = sent.reshape(32, KV).astype(f16)
    sent = jnp.broadcast_to(sent[None], (32, 32, KV))
    old_vecs = lax.dynamic_index_in_dim(parts, zh * 32 + owner_gain, 0, keepdims=False)
    old_vecs = old_vecs[EXTRA + 4 :].astype(f32) * (1.0 / 4096.0)
    old_vecs = lax.dynamic_slice_in_dim(old_vecs, x * 32, 32, 1)
    old_vecs = old_vecs[0::2] + old_vecs[1::2] * (1.0 / 256.0)
    first_row = rep * 1024 + place * 32
    grad_gain = lax.dynamic_slice_in_dim(lanes, x * 32, 32)

    gain_part = lax.dynamic_slice_in_dim(norm_gain, first_row, 32)
    gain_new = adam_step(gain_part, grad_gain, old_vecs[0], old_vecs[1], gain_rate)[0]
    gain_lanes = jnp.where(own_lanes, jnp.tile(gain_new, 4), jnp.zeros((), bf16))
    high = lax.reduce_precision(lanes, 8, 7)
    middle = lax.reduce_precision(lanes - high, 8, 7)
    rows = [gain_lanes, power, high, middle, lanes - high - middle]
    rows = jnp.stack([row.astype(bf16) for row in rows])
    arrived, grad_rows, sent, rows = lax.optimization_barrier((arrived, grad_rows, sent, rows))
    old_mats = last_picks[0]
    for k in range(1, 8):
        source = (zl * 4 + x) ^ k == (owner_weight & 7)
        old_mats = jnp.where(source, arrived[k - 1], old_mats)
    old_mats = old_mats.astype(f32)

    own_rows = blocked(lax.dynamic_slice_in_dim(value_weight, first_row, 32))
    weight_rows = adam_step(
        own_rows, grad_rows, blocked(old_mats[:32]), blocked(old_mats[32:]), learn_rate
    )[0]
    block = jnp.concatenate(
        [weight_rows, rows, jnp.zeros((ROWS - EXTRA - 5, 128), bf16)]
    )

    own = lax.all_to_all(
        jnp.broadcast_to(block[None], (64, ROWS, 128)), CHIPS, 0, 0, tiled=True
    )
    other = swap(own, 0, 1)
    grads = lax.all_to_all(sent, DP, 0, 0, tiled=True)

    value_ins = [
        pl.BlockSpec((16, ROWS, 128), lambda i, core: (i, 0, 0)),
        pl.BlockSpec((TOK, BLK), lambda i, core: (0, column(i, core))),
        whole((TOK, 128)),
    ]
    gain_spec = pl.BlockSpec((1, BLK), lambda i, core: (0, column(i, core)))
    any_spec = pl.BlockSpec(memory_space=pl.ANY)
    started, gain_started, acc = call(
        first_kernel,
        4,
        value_ins,
        (wide, gain_spec, whole((TOK, KV))),
        (shape((D, KV), bf16), shape((1, D), f32), shape((TOK, KV), f32)),
    )(core_at, own, next_hidden, next_inv)
    new_weight, new_gain, next_values = call(
        last_kernel,
        4,
        value_ins + [whole((TOK, KV)), any_spec, any_spec],
        (wide, gain_spec, whole((TOK, KV))),
        (shape((D, KV), bf16), shape((1, D), f32), shape((TOK, KV), bf16)),
        [pltpu.VMEM((TOK, KV), f32)],
        input_output_aliases={5: 0, 6: 1},
    )(other_at, other, next_hidden, next_inv, acc, started, gain_started)
    new_gain = new_gain.reshape(D).astype(bf16)

    ends = lax.dynamic_slice_in_dim(own[:, EXTRA + 1 : EXTRA + 5], zh * 32, 32).astype(f32)
    rep_gain = ends[:, 1] + ends[:, 2] + ends[:, 3]
    rep_gain = jnp.sum(rep_gain.reshape(8, 4, 128), axis=1).reshape(1, 1024)
    first_vec = beta_first * vec_first + (1.0 - beta_first) * rep_gain
    second_vec = beta_second * vec_second + (1.0 - beta_second) * rep_gain * rep_gain
    new_vec_first = jnp.where(holds_gain, first_vec, vec_first)
    new_vec_second = jnp.where(holds_gain, second_vec, vec_second)
    back = jnp.tile(jnp.exp2(-ends[:, 0]), (1, 4))
    grads, back, _ = lax.optimization_barrier((grads, back, next_values))
    rep_rows = grads.astype(f32) * back[:, None]
    old_first, old_second = mat_first.reshape(32, 32, KV), mat_second.reshape(32, 32, KV)
    first_mat = beta_first * old_first + (1.0 - beta_first) * rep_rows
    second_mat = beta_second * old_second + (1.0 - beta_second) * rep_rows * rep_rows
    new_mat_first = jnp.where(holds_weight, first_mat, old_first).reshape(1, 1024, KV)
    new_mat_second = jnp.where(holds_weight, second_mat, old_second).reshape(1, 1024, KV)
    return (
        new_weight,
        new_gain,
        new_mat_first,
        new_mat_second,
        new_vec_first,
        new_vec_second,
        next_values,
    )


def solution(mesh):
    fine = Mesh(mesh.devices.reshape(4, 2, 4, 2, 2), AXES)
    rep = ("zh", "c")
    tokens = P(AXES, None)
    return jax.shard_map(
        body,
        mesh=fine,
        in_specs=(
            tokens,
            tokens,
            P(),
            P(),
            P(),
            P(DP, rep, None),
            P(DP, rep, None),
            P(DP, rep),
            P(DP, rep),
            tokens,
        ),
        out_specs=(
            P(),
            P(),
            P(DP, rep, None),
            P(DP, rep, None),
            P(DP, rep),
            P(DP, rep),
            tokens,
        ),
        check_vma=False,
    )
```

```python
import jax
import jax.numpy as jnp
from jax import lax
from jax.experimental import pallas as pl
from jax.experimental.pallas import tpu as pltpu
from jax.sharding import Mesh, PartitionSpec as P

norm_eps = 1e-05
adam_eps = 1e-08
beta_first = 0.9
beta_second = 0.95
learn_rate = 0.001
gain_rate = 0.02
fix_first = 1.0 - 0.9**10
fix_second = 1.0 - 0.95**10

D, KV, TOK = 4096, 512, 768
BLK = 512
HALF = D // 2
ROWS = 136
EXTRA = 128
AXES = ("y", "zl", "x", "zh", "c")
CHIPS = ("zh", "y", "zl", "x")
DP = ("y", "zl", "x")
MOST = 149000.0
PARAMS = pltpu.CompilerParams(vmem_limit_bytes=50 * 1024 * 1024)
COST = pl.CostEstimate(flops=1, transcendentals=0, bytes_accessed=1)
f32, bf16, f16 = jnp.float32, jnp.bfloat16, jnp.float16


def pairs(mask, core=0):
    out = []
    for dev in range(128):
        chip = ((dev >> 1) & 1) * 32 + (dev >> 2)
        to = chip ^ mask
        out.append((dev, ((to & 31) << 2) + ((to >> 5) << 1) + ((dev & 1) ^ core)))
    return out


def swap(block, mask, core=0):
    return lax.ppermute(block, AXES, pairs(mask, core))


def adam_step(parameter, gradient, first_moment, second_moment, step_rate):
    first_moment = beta_first * first_moment + (1.0 - beta_first) * gradient
    second_moment = beta_second * second_moment + (1.0 - beta_second) * gradient * gradient
    update = first_moment / fix_first / (jnp.sqrt(second_moment / fix_second) + adam_eps)
    return (
        (parameter.astype(f32) - step_rate * update).astype(bf16),
        first_moment,
        second_moment,
    )


def hbm(x):
    return pltpu.with_memory_space_constraint(x, pltpu.HBM)


def fold(values):
    total = values[:, :128]
    for at in range(128, values.shape[1], 128):
        total = total + values[:, at : at + 128]
    return total


def inv_rms(hid):
    squares = jnp.zeros((hid.shape[0], 128), f32)
    for at in range(0, D, BLK):
        wide = hid[:, at : at + BLK].astype(f32)
        squares = squares + fold(wide * wide)
    mean = jnp.sum(squares, axis=1, keepdims=True) * (1.0 / D)
    return lax.rsqrt(mean + norm_eps)


def scale_kernel(core, hid, grad, out, theirs):
    most = jnp.max(jnp.abs(grad[...].astype(f32)), keepdims=True)
    lanes = lax.broadcasted_iota(jnp.int32, out.shape, 1)
    for half in range(2):
        start = pl.multiple_of((half * 2 + 1 - core[0]) * 1024, 1024)
        theirs[:, half * 1024 : half * 1024 + 1024] = hid[:, pl.ds(start, 1024)]
    out[...] = jnp.where(lanes < 64, inv_rms(hid), most)


def next_kernel(hid, out):
    out[...] = jnp.broadcast_to(inv_rms(hid), out.shape)


def products(hid, gain, grad, weight, inv):
    unit = hid[...].astype(f32) * inv[:, :1]
    normed = (unit * gain[...].astype(f32)).astype(bf16)
    part = lax.dot_general(
        normed, grad[...], (((0,), (0,)), ((), ())), preferred_element_type=f32
    )
    back = lax.dot_general(
        grad[...], weight[...], (((1,), (1,)), ((), ())), preferred_element_type=f32
    )
    return part, jnp.sum(back * unit, axis=0, keepdims=True)


def chip_kernel(core, hid, got_hid, gain, grad, got_grad, weight, inv, got_inv, firsts, seconds, out, after):
    after[...] = jnp.zeros_like(after)
    part, gain_part = products(hid, gain, grad, weight, inv)
    got_part, got_gain = products(got_hid, gain, got_grad, weight, got_inv)
    most = jnp.maximum(
        jnp.max(inv[:, 64:], keepdims=True), jnp.max(got_inv[:, 64:], keepdims=True)
    )
    power = jnp.floor(jnp.log(30000.0 / MOST / jnp.maximum(most, 1e-30)) * 1.4426950408889634)
    scale = jnp.exp(power * 0.6931471805599453)
    part = (part + got_part) * scale
    left = (gain_part + got_gain) * (scale * (1.0 / 64.0))
    pieces = []
    for step in (1.0, 256.0, 65536.0):
        rounded = left.astype(bf16).astype(f32)
        pieces.append(rounded * step)
        left = left - rounded
    vecs = []
    for vec in (firsts, seconds):
        whole_part = vec[...] * 4096.0
        rounded = whole_part.astype(bf16).astype(f32)
        vecs += [rounded, (whole_part - rounded) * 256.0]
    for j in range(BLK // 32):
        for b in range(4):
            out[j, b * 32 : b * 32 + 32, :] = part[j * 32 : j * 32 + 32, b * 128 : b * 128 + 128]
        lanes = slice((j // 4) * 128, (j // 4) * 128 + 128)
        rows = [piece[:, lanes] for piece in pieces] + [jnp.broadcast_to(power, (1, 128))]
        rows += [vec[:, lanes] for vec in vecs]
        out[j, EXTRA:, :] = jnp.concatenate(rows)


def value_step(blocks, hid, inv, weight, gain_out):
    lanes = []
    for j in range(BLK // 32):
        for b in range(4):
            weight[j * 32 : j * 32 + 32, b * 128 : b * 128 + 128] = blocks[
                j, b * 32 : b * 32 + 32, :
            ]
    for j in range(0, BLK // 32, 4):
        rows = [blocks[j + k, EXTRA : EXTRA + 8, :].astype(f32)[:1] for k in range(4)]
        lanes.append((rows[0] + rows[1]) + (rows[2] + rows[3]))
    gain = jnp.concatenate(lanes, axis=1)
    gain_out[...] = gain
    unit = hid[...].astype(f32) * inv[:, :1]
    normed = (unit * gain).astype(bf16)
    return jnp.dot(normed, weight[...], preferred_element_type=f32)


def first_kernel(core, blocks, hid, inv, weight, gain, out):
    part = value_step(blocks, hid, inv, weight, gain)

    @pl.when(pl.program_id(0) == 0)
    def _():
        out[...] = part

    @pl.when(pl.program_id(0) > 0)
    def _():
        out[...] += part


def last_kernel(core, blocks, hid, inv, acc, started, gain_started, weight, gain, out, total):
    part = value_step(blocks, hid, inv, weight, gain)

    @pl.when(pl.program_id(0) == 0)
    def _():
        total[...] = acc[...] + part

    @pl.when(pl.program_id(0) > 0)
    def _():
        total[...] += part

    @pl.when(pl.program_id(0) == pl.num_programs(0) - 1)
    def _():
        out[...] = total[...].astype(bf16)


def shape(dims, dtype):
    return jax.ShapeDtypeStruct(dims, dtype)


def whole(dims):
    return pl.BlockSpec(dims, lambda i, *_: (0,) * len(dims))


def column(i, core):
    return ((i // 2) * 2 + core[0]) * 2 + i % 2


def call(kernel, grid, ins, outs, out_shape, scratch=(), prefetch=1, params=PARAMS, **more):
    return pl.pallas_call(
        kernel,
        grid_spec=pltpu.PrefetchScalarGridSpec(
            num_scalar_prefetch=prefetch,
            grid=(grid,),
            in_specs=ins,
            out_specs=outs,
            scratch_shapes=scratch,
        ),
        out_shape=out_shape,
        compiler_params=params,
        cost_estimate=COST,
        **more,
    )


def blocked(rows):
    return rows.reshape(32, 4, 128).transpose(1, 0, 2).reshape(128, 128)


def body(
    hidden_in,
    value_grad,
    value_weight,
    norm_gain,
    owner_map,
    mat_first,
    mat_second,
    vec_first,
    vec_second,
    next_hidden,
):
    y, zl, x = lax.axis_index("y"), lax.axis_index("zl"), lax.axis_index("x")
    zh, core = lax.axis_index("zh"), lax.axis_index("c")
    place = y * 8 + zl * 4 + x
    rep = zh * 2 + core
    owner_weight, owner_gain = owner_map[0], owner_map[1]
    holds_weight = place == owner_weight
    holds_gain = place == owner_gain
    core_at, other_at = core.reshape(1), (1 - core).reshape(1)
    gain_row = norm_gain.reshape(1, D)

    hid_spec = pl.BlockSpec((TOK, BLK), lambda i, core: (0, column(i, core)))
    inv, theirs = call(
        scale_kernel,
        2,
        [
            pl.BlockSpec((384, D), lambda i, core: (i, 0)),
            pl.BlockSpec((384, KV), lambda i, core: (i, 0)),
        ],
        (
            pl.BlockSpec((384, 128), lambda i, core: (i, 0)),
            pl.BlockSpec((384, HALF), lambda i, core: (i, 0)),
        ),
        (shape((TOK, 128), f32), shape((TOK, HALF), bf16)),
    )(core_at, hidden_in, value_grad)
    got_hid, got_grad, got_inv = swap(theirs, 0, 1), swap(value_grad, 0, 1), swap(inv, 0, 1)

    def share(picks, at, source, unit):
        kept = picks[0]
        for k in range(1, len(picks)):
            kept = jnp.where((at ^ k) == source, swap(picks[k], k * unit), kept)
        return kept

    def first_pick(k):
        return jnp.concatenate(
            [
                lax.dynamic_slice_in_dim(m[0], (y ^ k) * 256, 256).astype(f16)
                for m in (mat_first, mat_second)
            ]
        )

    first_picks = [first_pick(k) for k in range(4)]

    side = pl.BlockSpec((1, BLK), lambda i, core: (0, column(i, core)))
    wide = pl.BlockSpec((BLK, KV), lambda i, core: (column(i, core), 0))
    scaled, after = call(
        chip_kernel,
        4,
        [
            hid_spec,
            pl.BlockSpec((TOK, BLK), lambda i, core: (0, i)),
            side,
            whole((TOK, KV)),
            whole((TOK, KV)),
            wide,
            whole((TOK, 128)),
            whole((TOK, 128)),
            pl.BlockSpec((1, BLK), lambda i, core: (0, i % 2)),
            pl.BlockSpec((1, BLK), lambda i, core: (0, i % 2)),
        ],
        (pl.BlockSpec((16, ROWS, 128), lambda i, core: (i, 0, 0)), whole((1, KV))),
        (shape((64, ROWS, 128), f32), shape((1, KV), f32)),
        params=pltpu.CompilerParams(vmem_limit_bytes=40 * 1024 * 1024),
    )(
        core_at,
        hbm(hidden_in),
        hbm(got_hid),
        gain_row,
        hbm(value_grad),
        hbm(got_grad),
        hbm(value_weight),
        hbm(inv),
        hbm(got_inv),
        vec_first,
        vec_second,
    )
    moments = share(first_picks, y, owner_weight >> 3, 8) + after.astype(f16)
    next_inv = pl.pallas_call(
        next_kernel,
        grid=(3,),
        in_specs=[pl.BlockSpec((256, D), lambda i: (i, 0))],
        out_specs=pl.BlockSpec((256, 128), lambda i: (i, 0)),
        out_shape=shape((TOK, 128), f32),
        compiler_params=PARAMS,
        cost_estimate=pl.CostEstimate(flops=17 * 10**9, transcendentals=0, bytes_accessed=1),
    )(lax.optimization_barrier((next_hidden, moments))[0])
    moments, next_inv = lax.optimization_barrier((moments, next_inv))
    moments = moments.reshape(2, 8, 32, KV)
    last_picks = [
        lax.dynamic_index_in_dim(moments, (zl * 4 + x) ^ k, 1, keepdims=False).reshape(64, KV)
        for k in range(8)
    ]
    arrived = [swap(last_picks[k], k) for k in range(1, 8)]

    parts = lax.all_to_all(scaled.astype(f16), CHIPS, 0, 0, tiled=True)
    parts, early = lax.optimization_barrier((parts, arrived[:5]))
    arrived = early + arrived[5:]
    back = jnp.exp2(-parts[:, EXTRA + 3].astype(f32))
    summed = jnp.sum(parts.astype(f32) * back[:, None], axis=0)
    grad_rows = summed[:EXTRA]
    lanes = summed[EXTRA] * 64.0 + summed[EXTRA + 1] * (64.0 / 256.0)
    lanes = lanes + summed[EXTRA + 2] * (64.0 / 65536.0)
    own_lanes = (jnp.arange(128) >> 5) == x
    lanes = jnp.where(own_lanes, lanes, 0.0)
    most = jnp.maximum(jnp.max(jnp.abs(grad_rows), axis=0), 1e-30)
    power = jnp.floor(jnp.log2(16384.0 / most))
    sent = (grad_rows * jnp.exp2(power)).reshape(4, 32, 128).transpose(1, 0, 2)
    sent = sent.reshape(32, KV).astype(f16)
    sent = jnp.broadcast_to(sent[None], (32, 32, KV))
    old_vecs = lax.dynamic_index_in_dim(parts, zh * 32 + owner_gain, 0, keepdims=False)
    old_vecs = old_vecs[EXTRA + 4 :].astype(f32) * (1.0 / 4096.0)
    old_vecs = lax.dynamic_slice_in_dim(old_vecs, x * 32, 32, 1)
    old_vecs = old_vecs[0::2] + old_vecs[1::2] * (1.0 / 256.0)
    first_row = rep * 1024 + place * 32
    grad_gain = lax.dynamic_slice_in_dim(lanes, x * 32, 32)

    gain_part = lax.dynamic_slice_in_dim(norm_gain, first_row, 32)
    gain_new = adam_step(gain_part, grad_gain, old_vecs[0], old_vecs[1], gain_rate)[0]
    gain_lanes = jnp.where(own_lanes, jnp.tile(gain_new, 4), jnp.zeros((), bf16))
    high = lax.reduce_precision(lanes, 8, 7)
    middle = lax.reduce_precision(lanes - high, 8, 7)
    rows = [gain_lanes, power, high, middle, lanes - high - middle]
    rows = jnp.stack([row.astype(bf16) for row in rows])
    arrived, grad_rows, sent, rows = lax.optimization_barrier((arrived, grad_rows, sent, rows))
    old_mats = last_picks[0]
    for k in range(1, 8):
        source = (zl * 4 + x) ^ k == (owner_weight & 7)
        old_mats = jnp.where(source, arrived[k - 1], old_mats)
    old_mats = old_mats.astype(f32)

    own_rows = blocked(lax.dynamic_slice_in_dim(value_weight, first_row, 32))
    weight_rows = adam_step(
        own_rows, grad_rows, blocked(old_mats[:32]), blocked(old_mats[32:]), learn_rate
    )[0]
    block = jnp.concatenate(
        [weight_rows, rows, jnp.zeros((ROWS - EXTRA - 5, 128), bf16)]
    )

    own = lax.all_to_all(
        jnp.broadcast_to(block[None], (64, ROWS, 128)), CHIPS, 0, 0, tiled=True
    )
    other = swap(own, 0, 1)
    grads = lax.all_to_all(sent, DP, 0, 0, tiled=True)

    value_ins = [
        pl.BlockSpec((16, ROWS, 128), lambda i, core: (i, 0, 0)),
        pl.BlockSpec((TOK, BLK), lambda i, core: (0, column(i, core))),
        whole((TOK, 128)),
    ]
    gain_spec = pl.BlockSpec((1, BLK), lambda i, core: (0, column(i, core)))
    any_spec = pl.BlockSpec(memory_space=pl.ANY)
    started, gain_started, acc = call(
        first_kernel,
        4,
        value_ins,
        (wide, gain_spec, whole((TOK, KV))),
        (shape((D, KV), bf16), shape((1, D), f32), shape((TOK, KV), f32)),
    )(core_at, own, next_hidden, next_inv)
    new_weight, new_gain, next_values = call(
        last_kernel,
        4,
        value_ins + [whole((TOK, KV)), any_spec, any_spec],
        (wide, gain_spec, whole((TOK, KV))),
        (shape((D, KV), bf16), shape((1, D), f32), shape((TOK, KV), bf16)),
        [pltpu.VMEM((TOK, KV), f32)],
        input_output_aliases={5: 0, 6: 1},
    )(other_at, other, next_hidden, next_inv, acc, started, gain_started)
    new_gain = new_gain.reshape(D).astype(bf16)

    ends = lax.dynamic_slice_in_dim(own[:, EXTRA + 1 : EXTRA + 5], zh * 32, 32).astype(f32)
    rep_gain = ends[:, 1] + ends[:, 2] + ends[:, 3]
    rep_gain = jnp.sum(rep_gain.reshape(8, 4, 128), axis=1).reshape(1, 1024)
    first_vec = beta_first * vec_first + (1.0 - beta_first) * rep_gain
    second_vec = beta_second * vec_second + (1.0 - beta_second) * rep_gain * rep_gain
    new_vec_first = jnp.where(holds_gain, first_vec, vec_first)
    new_vec_second = jnp.where(holds_gain, second_vec, vec_second)
    back = jnp.tile(jnp.exp2(-ends[:, 0]), (1, 4))
    grads, back, new_gain = lax.optimization_barrier((grads, back, new_gain))
    rep_rows = grads.astype(f32) * back[:, None]
    old_first, old_second = mat_first.reshape(32, 32, KV), mat_second.reshape(32, 32, KV)
    first_mat = beta_first * old_first + (1.0 - beta_first) * rep_rows
    second_mat = beta_second * old_second + (1.0 - beta_second) * rep_rows * rep_rows
    new_mat_first = jnp.where(holds_weight, first_mat, old_first).reshape(1, 1024, KV)
    new_mat_second = jnp.where(holds_weight, second_mat, old_second).reshape(1, 1024, KV)
    return (
        new_weight,
        new_gain,
        new_mat_first,
        new_mat_second,
        new_vec_first,
        new_vec_second,
        next_values,
    )


def solution(mesh):
    fine = Mesh(mesh.devices.reshape(4, 2, 4, 2, 2), AXES)
    rep = ("zh", "c")
    tokens = P(AXES, None)
    return jax.shard_map(
        body,
        mesh=fine,
        in_specs=(
            tokens,
            tokens,
            P(),
            P(),
            P(),
            P(DP, rep, None),
            P(DP, rep, None),
            P(DP, rep),
            P(DP, rep),
            tokens,
        ),
        out_specs=(
            P(),
            P(),
            P(DP, rep, None),
            P(DP, rep, None),
            P(DP, rep),
            P(DP, rep),
            tokens,
        ),
        check_vma=False,
    )
```

```python
import jax
import jax.numpy as jnp
from jax import lax
from jax.experimental import pallas as pl
from jax.experimental.pallas import tpu as pltpu
from jax.sharding import Mesh, PartitionSpec as P

norm_eps = 1e-05
adam_eps = 1e-08
beta_first = 0.9
beta_second = 0.95
learn_rate = 0.001
gain_rate = 0.02
fix_first = 1.0 - 0.9**10
fix_second = 1.0 - 0.95**10

D, KV, TOK = 4096, 512, 768
BLK = 512
HALF = D // 2
ROWS = 136
EXTRA = 128
AXES = ("y", "zl", "x", "zh", "c")
CHIPS = ("zh", "y", "zl", "x")
DP = ("y", "zl", "x")
MOST = 149000.0
PARAMS = pltpu.CompilerParams(vmem_limit_bytes=50 * 1024 * 1024)
COST = pl.CostEstimate(flops=1, transcendentals=0, bytes_accessed=1)
f32, bf16, f16 = jnp.float32, jnp.bfloat16, jnp.float16


def pairs(mask, core=0):
    out = []
    for dev in range(128):
        chip = ((dev >> 1) & 1) * 32 + (dev >> 2)
        to = chip ^ mask
        out.append((dev, ((to & 31) << 2) + ((to >> 5) << 1) + ((dev & 1) ^ core)))
    return out


def swap(block, mask, core=0):
    return lax.ppermute(block, AXES, pairs(mask, core))


def adam_step(parameter, gradient, first_moment, second_moment, step_rate):
    first_moment = beta_first * first_moment + (1.0 - beta_first) * gradient
    second_moment = beta_second * second_moment + (1.0 - beta_second) * gradient * gradient
    update = first_moment / fix_first / (jnp.sqrt(second_moment / fix_second) + adam_eps)
    return (
        (parameter.astype(f32) - step_rate * update).astype(bf16),
        first_moment,
        second_moment,
    )


def hbm(x):
    return pltpu.with_memory_space_constraint(x, pltpu.HBM)


def fold(values):
    total = values[:, :128]
    for at in range(128, values.shape[1], 128):
        total = total + values[:, at : at + 128]
    return total


def inv_rms(hid):
    squares = jnp.zeros((hid.shape[0], 128), f32)
    for at in range(0, D, BLK):
        wide = hid[:, at : at + BLK].astype(f32)
        squares = squares + fold(wide * wide)
    mean = jnp.sum(squares, axis=1, keepdims=True) * (1.0 / D)
    return lax.rsqrt(mean + norm_eps)


def scale_kernel(core, hid, grad, out, theirs):
    most = jnp.max(jnp.abs(grad[...].astype(f32)), keepdims=True)
    lanes = lax.broadcasted_iota(jnp.int32, out.shape, 1)
    for half in range(2):
        start = pl.multiple_of((half * 2 + 1 - core[0]) * 1024, 1024)
        theirs[:, half * 1024 : half * 1024 + 1024] = hid[:, pl.ds(start, 1024)]
    out[...] = jnp.where(lanes < 64, inv_rms(hid), most)


def next_kernel(hid, out):
    out[...] = jnp.broadcast_to(inv_rms(hid), out.shape)


def products(hid, gain, grad, weight, inv):
    unit = hid[...].astype(f32) * inv[:, :1]
    normed = (unit * gain[...].astype(f32)).astype(bf16)
    part = lax.dot_general(
        normed, grad[...], (((0,), (0,)), ((), ())), preferred_element_type=f32
    )
    back = lax.dot_general(
        grad[...], weight[...], (((1,), (1,)), ((), ())), preferred_element_type=f32
    )
    return part, jnp.sum(back * unit, axis=0, keepdims=True)


def chip_kernel(core, hid, got_hid, gain, grad, got_grad, weight, inv, got_inv, firsts, seconds, out, after):
    after[...] = jnp.zeros_like(after)
    part, gain_part = products(hid, gain, grad, weight, inv)
    got_part, got_gain = products(got_hid, gain, got_grad, weight, got_inv)
    most = jnp.maximum(
        jnp.max(inv[:, 64:], keepdims=True), jnp.max(got_inv[:, 64:], keepdims=True)
    )
    power = jnp.floor(jnp.log(30000.0 / MOST / jnp.maximum(most, 1e-30)) * 1.4426950408889634)
    scale = jnp.exp(power * 0.6931471805599453)
    part = (part + got_part) * scale
    left = (gain_part + got_gain) * (scale * (1.0 / 64.0))
    pieces = []
    for step in (1.0, 256.0, 65536.0):
        rounded = left.astype(bf16).astype(f32)
        pieces.append(rounded * step)
        left = left - rounded
    vecs = []
    for vec in (firsts, seconds):
        whole_part = vec[...] * 4096.0
        rounded = whole_part.astype(bf16).astype(f32)
        vecs += [rounded, (whole_part - rounded) * 256.0]
    for j in range(BLK // 32):
        for b in range(4):
            out[j, b * 32 : b * 32 + 32, :] = part[j * 32 : j * 32 + 32, b * 128 : b * 128 + 128]
        lanes = slice((j // 4) * 128, (j // 4) * 128 + 128)
        rows = [piece[:, lanes] for piece in pieces] + [jnp.broadcast_to(power, (1, 128))]
        rows += [vec[:, lanes] for vec in vecs]
        out[j, EXTRA:, :] = jnp.concatenate(rows)


def value_step(blocks, hid, inv, weight, gain_out):
    lanes = []
    for j in range(BLK // 32):
        for b in range(4):
            weight[j * 32 : j * 32 + 32, b * 128 : b * 128 + 128] = blocks[
                j, b * 32 : b * 32 + 32, :
            ]
    for j in range(0, BLK // 32, 4):
        rows = [blocks[j + k, EXTRA : EXTRA + 8, :].astype(f32)[:1] for k in range(4)]
        lanes.append((rows[0] + rows[1]) + (rows[2] + rows[3]))
    gain = jnp.concatenate(lanes, axis=1)
    gain_out[...] = gain
    unit = hid[...].astype(f32) * inv[:, :1]
    normed = (unit * gain).astype(bf16)
    return jnp.dot(normed, weight[...], preferred_element_type=f32)


def first_kernel(core, blocks, hid, inv, weight, gain, out):
    part = value_step(blocks, hid, inv, weight, gain)

    @pl.when(pl.program_id(0) == 0)
    def _():
        out[...] = part

    @pl.when(pl.program_id(0) > 0)
    def _():
        out[...] += part


def last_kernel(core, blocks, hid, inv, acc, started, gain_started, weight, gain, out, total):
    part = value_step(blocks, hid, inv, weight, gain)

    @pl.when(pl.program_id(0) == 0)
    def _():
        total[...] = acc[...] + part

    @pl.when(pl.program_id(0) > 0)
    def _():
        total[...] += part

    @pl.when(pl.program_id(0) == pl.num_programs(0) - 1)
    def _():
        out[...] = total[...].astype(bf16)


def shape(dims, dtype):
    return jax.ShapeDtypeStruct(dims, dtype)


def whole(dims):
    return pl.BlockSpec(dims, lambda i, *_: (0,) * len(dims))


def column(i, core):
    return ((i // 2) * 2 + core[0]) * 2 + i % 2


def call(kernel, grid, ins, outs, out_shape, scratch=(), prefetch=1, params=PARAMS, **more):
    return pl.pallas_call(
        kernel,
        grid_spec=pltpu.PrefetchScalarGridSpec(
            num_scalar_prefetch=prefetch,
            grid=(grid,),
            in_specs=ins,
            out_specs=outs,
            scratch_shapes=scratch,
        ),
        out_shape=out_shape,
        compiler_params=params,
        cost_estimate=COST,
        **more,
    )


def blocked(rows):
    return rows.reshape(32, 4, 128).transpose(1, 0, 2).reshape(128, 128)


def body(
    hidden_in,
    value_grad,
    value_weight,
    norm_gain,
    owner_map,
    mat_first,
    mat_second,
    vec_first,
    vec_second,
    next_hidden,
):
    y, zl, x = lax.axis_index("y"), lax.axis_index("zl"), lax.axis_index("x")
    zh, core = lax.axis_index("zh"), lax.axis_index("c")
    place = y * 8 + zl * 4 + x
    rep = zh * 2 + core
    owner_weight, owner_gain = owner_map[0], owner_map[1]
    holds_weight = place == owner_weight
    holds_gain = place == owner_gain
    core_at, other_at = core.reshape(1), (1 - core).reshape(1)
    gain_row = norm_gain.reshape(1, D)

    hid_spec = pl.BlockSpec((TOK, BLK), lambda i, core: (0, column(i, core)))
    inv, theirs = call(
        scale_kernel,
        2,
        [
            pl.BlockSpec((384, D), lambda i, core: (i, 0)),
            pl.BlockSpec((384, KV), lambda i, core: (i, 0)),
        ],
        (
            pl.BlockSpec((384, 128), lambda i, core: (i, 0)),
            pl.BlockSpec((384, HALF), lambda i, core: (i, 0)),
        ),
        (shape((TOK, 128), f32), shape((TOK, HALF), bf16)),
    )(core_at, hidden_in, value_grad)
    got_hid, got_grad, got_inv = swap(theirs, 0, 1), swap(value_grad, 0, 1), swap(inv, 0, 1)

    def share(picks, at, source, unit):
        kept = picks[0]
        for k in range(1, len(picks)):
            kept = jnp.where((at ^ k) == source, swap(picks[k], k * unit), kept)
        return kept

    def first_pick(k):
        return jnp.concatenate(
            [
                lax.dynamic_slice_in_dim(m[0], (y ^ k) * 256, 256).astype(f16)
                for m in (mat_first, mat_second)
            ]
        )

    first_picks = [first_pick(k) for k in range(4)]

    side = pl.BlockSpec((1, BLK), lambda i, core: (0, column(i, core)))
    wide = pl.BlockSpec((BLK, KV), lambda i, core: (column(i, core), 0))
    scaled, after = call(
        chip_kernel,
        4,
        [
            hid_spec,
            pl.BlockSpec((TOK, BLK), lambda i, core: (0, i)),
            side,
            whole((TOK, KV)),
            whole((TOK, KV)),
            wide,
            whole((TOK, 128)),
            whole((TOK, 128)),
            pl.BlockSpec((1, BLK), lambda i, core: (0, i % 2)),
            pl.BlockSpec((1, BLK), lambda i, core: (0, i % 2)),
        ],
        (pl.BlockSpec((16, ROWS, 128), lambda i, core: (i, 0, 0)), whole((1, KV))),
        (shape((64, ROWS, 128), f32), shape((1, KV), f32)),
        params=pltpu.CompilerParams(vmem_limit_bytes=40 * 1024 * 1024),
    )(
        core_at,
        hbm(hidden_in),
        hbm(got_hid),
        gain_row,
        hbm(value_grad),
        hbm(got_grad),
        hbm(value_weight),
        hbm(inv),
        hbm(got_inv),
        vec_first,
        vec_second,
    )
    moments = share(first_picks, y, owner_weight >> 3, 8) + after.astype(f16)
    next_inv = pl.pallas_call(
        next_kernel,
        grid=(3,),
        in_specs=[pl.BlockSpec((256, D), lambda i: (i, 0))],
        out_specs=pl.BlockSpec((256, 128), lambda i: (i, 0)),
        out_shape=shape((TOK, 128), f32),
        compiler_params=PARAMS,
        cost_estimate=pl.CostEstimate(flops=17 * 10**9, transcendentals=0, bytes_accessed=1),
    )(lax.optimization_barrier((next_hidden, moments))[0])
    moments, next_inv = lax.optimization_barrier((moments, next_inv))
    moments = moments.reshape(2, 2, 4, 32, KV)
    near = [lax.dynamic_index_in_dim(moments, x ^ k, 2, keepdims=False) for k in range(4)]
    arrived = [swap(near[k], k) for k in range(1, 4)]

    parts = lax.all_to_all(scaled.astype(f16), CHIPS, 0, 0, tiled=True)
    parts, arrived = lax.optimization_barrier((parts, arrived))
    near = near[0]
    for k in range(1, 4):
        near = jnp.where((x ^ k) == (owner_weight & 3), arrived[k - 1], near)
    kept, passed = [lax.dynamic_index_in_dim(near, zl ^ k, 1, keepdims=False) for k in range(2)]
    arrived = swap(passed, 4)
    back = jnp.exp2(-parts[:, EXTRA + 3].astype(f32))
    summed = jnp.sum(parts.astype(f32) * back[:, None], axis=0)
    grad_rows = summed[:EXTRA]
    lanes = summed[EXTRA] * 64.0 + summed[EXTRA + 1] * (64.0 / 256.0)
    lanes = lanes + summed[EXTRA + 2] * (64.0 / 65536.0)
    own_lanes = (jnp.arange(128) >> 5) == x
    lanes = jnp.where(own_lanes, lanes, 0.0)
    most = jnp.maximum(jnp.max(jnp.abs(grad_rows), axis=0), 1e-30)
    power = jnp.floor(jnp.log2(16384.0 / most))
    sent = (grad_rows * jnp.exp2(power)).reshape(4, 32, 128).transpose(1, 0, 2)
    sent = sent.reshape(32, KV).astype(f16)
    sent = jnp.broadcast_to(sent[None], (32, 32, KV))
    old_vecs = lax.dynamic_index_in_dim(parts, zh * 32 + owner_gain, 0, keepdims=False)
    old_vecs = old_vecs[EXTRA + 4 :].astype(f32) * (1.0 / 4096.0)
    old_vecs = lax.dynamic_slice_in_dim(old_vecs, x * 32, 32, 1)
    old_vecs = old_vecs[0::2] + old_vecs[1::2] * (1.0 / 256.0)
    first_row = rep * 1024 + place * 32
    grad_gain = lax.dynamic_slice_in_dim(lanes, x * 32, 32)

    gain_part = lax.dynamic_slice_in_dim(norm_gain, first_row, 32)
    gain_new = adam_step(gain_part, grad_gain, old_vecs[0], old_vecs[1], gain_rate)[0]
    gain_lanes = jnp.where(own_lanes, jnp.tile(gain_new, 4), jnp.zeros((), bf16))
    high = lax.reduce_precision(lanes, 8, 7)
    middle = lax.reduce_precision(lanes - high, 8, 7)
    rows = [gain_lanes, power, high, middle, lanes - high - middle]
    rows = jnp.stack([row.astype(bf16) for row in rows])
    arrived, grad_rows, sent, rows = lax.optimization_barrier((arrived, grad_rows, sent, rows))
    old_mats = jnp.where(((owner_weight >> 2) & 1) == zl, kept, arrived).reshape(64, KV)
    old_mats = old_mats.astype(f32)

    own_rows = blocked(lax.dynamic_slice_in_dim(value_weight, first_row, 32))
    weight_rows = adam_step(
        own_rows, grad_rows, blocked(old_mats[:32]), blocked(old_mats[32:]), learn_rate
    )[0]
    block = jnp.concatenate(
        [weight_rows, rows, jnp.zeros((ROWS - EXTRA - 5, 128), bf16)]
    )

    own = lax.all_to_all(
        jnp.broadcast_to(block[None], (64, ROWS, 128)), CHIPS, 0, 0, tiled=True
    )
    other = swap(own, 0, 1)
    grads = lax.all_to_all(sent, DP, 0, 0, tiled=True)

    value_ins = [
        pl.BlockSpec((16, ROWS, 128), lambda i, core: (i, 0, 0)),
        pl.BlockSpec((TOK, BLK), lambda i, core: (0, column(i, core))),
        whole((TOK, 128)),
    ]
    gain_spec = pl.BlockSpec((1, BLK), lambda i, core: (0, column(i, core)))
    any_spec = pl.BlockSpec(memory_space=pl.ANY)
    started, gain_started, acc = call(
        first_kernel,
        4,
        value_ins,
        (wide, gain_spec, whole((TOK, KV))),
        (shape((D, KV), bf16), shape((1, D), f32), shape((TOK, KV), f32)),
    )(core_at, own, next_hidden, next_inv)
    new_weight, new_gain, next_values = call(
        last_kernel,
        4,
        value_ins + [whole((TOK, KV)), any_spec, any_spec],
        (wide, gain_spec, whole((TOK, KV))),
        (shape((D, KV), bf16), shape((1, D), f32), shape((TOK, KV), bf16)),
        [pltpu.VMEM((TOK, KV), f32)],
        input_output_aliases={5: 0, 6: 1},
    )(other_at, other, next_hidden, next_inv, acc, started, gain_started)
    new_gain = new_gain.reshape(D).astype(bf16)

    ends = lax.dynamic_slice_in_dim(own[:, EXTRA + 1 : EXTRA + 5], zh * 32, 32).astype(f32)
    rep_gain = ends[:, 1] + ends[:, 2] + ends[:, 3]
    rep_gain = jnp.sum(rep_gain.reshape(8, 4, 128), axis=1).reshape(1, 1024)
    first_vec = beta_first * vec_first + (1.0 - beta_first) * rep_gain
    second_vec = beta_second * vec_second + (1.0 - beta_second) * rep_gain * rep_gain
    new_vec_first = jnp.where(holds_gain, first_vec, vec_first)
    new_vec_second = jnp.where(holds_gain, second_vec, vec_second)
    back = jnp.tile(jnp.exp2(-ends[:, 0]), (1, 4))
    grads, back, new_gain = lax.optimization_barrier((grads, back, new_gain))
    rep_rows = grads.astype(f32) * back[:, None]
    old_first, old_second = mat_first.reshape(32, 32, KV), mat_second.reshape(32, 32, KV)
    first_mat = beta_first * old_first + (1.0 - beta_first) * rep_rows
    second_mat = beta_second * old_second + (1.0 - beta_second) * rep_rows * rep_rows
    new_mat_first = jnp.where(holds_weight, first_mat, old_first).reshape(1, 1024, KV)
    new_mat_second = jnp.where(holds_weight, second_mat, old_second).reshape(1, 1024, KV)
    return (
        new_weight,
        new_gain,
        new_mat_first,
        new_mat_second,
        new_vec_first,
        new_vec_second,
        next_values,
    )


def solution(mesh):
    fine = Mesh(mesh.devices.reshape(4, 2, 4, 2, 2), AXES)
    rep = ("zh", "c")
    tokens = P(AXES, None)
    return jax.shard_map(
        body,
        mesh=fine,
        in_specs=(
            tokens,
            tokens,
            P(),
            P(),
            P(),
            P(DP, rep, None),
            P(DP, rep, None),
            P(DP, rep),
            P(DP, rep),
            tokens,
        ),
        out_specs=(
            P(),
            P(),
            P(DP, rep, None),
            P(DP, rep, None),
            P(DP, rep),
            P(DP, rep),
            tokens,
        ),
        check_vma=False,
    )
```
